512 devices in a mesh: fft: 32 (over x, z), band: 16 (over y, core).
Axes of the slice: x: 4, y: 8, z: 8, core: 2. Of those that a mesh axis runs over, the one named last changes fastest.
Arguments:
- psi_real: float32 [16, 64, 64, 128], P('band', 'fft'), may hold values from -6 to 6
- psi_imag: float32 [16, 64, 64, 128], P('band', 'fft'), may hold values from -6 to 6
- potential: float32 [64, 64, 128], P('fft'), may hold values from -3 to 3
- vector_potential: float32 [3], replicated, may hold values from -2 to 2
- occupation: float32 [16], P('band'), may hold values from 0.2 to 2
- projectors: float32 [128, 8, 4096], P('fft'), may hold values from -1.5 to 1.5
- box_offsets: int32 [3, 128], P(None, 'fft'), may hold values from 0 to 127, as said below
- species: int32 [128], P('fft'), may hold values from 0 to 3
- channels: int32 [128, 8], P('fft'), may hold values 0 or 1
- coupling: float32 [4, 8, 8], replicated, may hold values from -8 to 8
Outputs:
- new_real: float32 [16, 64, 64, 128], P('band', 'fft')
- new_imag: float32 [16, 64, 64, 128], P('band', 'fft')
- density: float32 [64, 64, 128], P('fft', 'band')
The draws below stay inside these ranges and needn't reach their ends.
Inputs may be any that keep to these rules, and one draw needn't show every extreme that they name: Atom a's box starts in slab a // 4: (a // 4) * 2 <= box_offsets[0, a] < (a // 4 + 1) * 2; box_offsets[1, a] < 64 and box_offsets[2, a] < 128. Both ends of the range are reached.
All inputs are finite; a program needn't handle non-finite values. No bound on the sum of `channels` on one device may be relied on, other than what follows from the above.
Results may differ from the reference program's by a relative error of at most 0.00011.
Values sent between devices are 32-bit elements; how exact they have to be, the bound alone decides.
No kernel may reach another device: no remote copies, remote signals or barrier semaphores. Data moves between devices by JAX's collectives and lax.ppermute only.
A program may use at most 64 MiB of HBM per device.

```python
import math
import jax
import jax.numpy as jnp
from jax import lax

NX = 64
NY = 64
NZ = 128
BX = 16
BY = 16
BZ = 16
NPROJ = 8
SPECIES = 4
ATOM_DEV = 4
CX = 2
ORBITALS = 16
ATOMS = 128
BOXC = 4096


def draw_box_offsets(key, part):
    key = jax.random.fold_in(key, 11)
    keys = jax.random.split(key, 3)
    owner = jnp.arange(ATOMS, dtype=jnp.int32) // ATOM_DEV
    start_x = owner * CX + jax.random.randint(keys[0], (ATOMS,), 0, CX)
    start_y = jax.random.randint(keys[1], (ATOMS,), 0, NY)
    start_z = jax.random.randint(keys[2], (ATOMS,), 0, NZ)
    start_x = start_x.at[0].set(0).at[ATOMS - 1].set(NX - 1)
    start_y = start_y.at[0].set(0).at[ATOMS - 1].set(NY - 1)
    start_z = start_z.at[0].set(0).at[ATOMS - 1].set(NZ - 1)
    return jnp.stack([start_x, start_y, start_z]).astype(jnp.int32)


def place_ends(values, own_key, least, largest):
    longest = values.shape.index(max(values.shape))
    spots = []
    for shift in (0, 1):
        where = [jax.random.randint(jax.random.fold_in(own_key, axis), (), 0, length) for axis, length in enumerate(values.shape)]
        where[longest] = (where[longest] + shift) % values.shape[longest]
        spots.append(tuple(where))
    return values.at[spots[0]].set(least).at[spots[1]].set(largest)


def block_scale(stream_key, shape, cuts, smallest, high):
    def one(dim, shards_of):
        steps = jax.random.uniform(jax.random.fold_in(jax.random.fold_in(stream_key, 6), dim), (shards_of,), jnp.float32, smallest / len(cuts), high / len(cuts))
        return jnp.repeat(jnp.exp(steps), shape[dim] // shards_of).reshape((-1,) + (1,) * (len(shape) - dim - 1))

    factor_of = one(*cuts[0])
    for cut in cuts[1:]:
        factor_of = factor_of * one(*cut)
    return factor_of


def noise(stream_key, extent, deviation, reach, pieces=(), kind=jnp.bfloat16):
    drawn = jax.random.normal(stream_key, extent, jnp.float32) * deviation
    if len(pieces) > 0:
        drawn = block_scale(stream_key, extent, pieces, -0.22, 0.18) * drawn
    return jnp.clip(drawn, min=-reach, max=reach).astype(kind)


def setup_inputs(seed: int = 0) -> dict:
    streams_of = jax.random.split(jax.random.key(seed), 11)
    return {
        "psi_real": noise(streams_of[0], (ORBITALS, NX, NY, NZ), 1.0, 6.0, ((0, 16), (1, 32)), jnp.float32),
        "psi_imag": noise(streams_of[1], (ORBITALS, NX, NY, NZ), 1.0, 6.0, ((0, 16), (1, 32)), jnp.float32),
        "potential": jnp.clip(jax.random.uniform(streams_of[2], (NX, NY, NZ), jnp.float32, -3.0, 3.0) * block_scale(streams_of[2], (NX, NY, NZ), ((0, 32),), -0.4, 0.0), -3.0, 3.0),
        "vector_potential": jnp.clip(jax.random.uniform(streams_of[3], (3,), jnp.float32, -2.0, 2.0), -2.0, 2.0),
        "occupation": jnp.clip(0.2 + 1.8 * jax.random.uniform(streams_of[4], (ORBITALS,), jnp.float32) ** block_scale(streams_of[4], (ORBITALS,), ((0, 16),), -0.2, 0.2), 0.2, 2.0),
        "projectors": noise(streams_of[5], (ATOMS, NPROJ, BOXC), 0.25, 1.5, ((0, 32),), jnp.float32),
        "box_offsets": draw_box_offsets(jax.random.fold_in(streams_of[10], 71), 0),
        "species": place_ends(jax.random.randint(streams_of[7], (ATOMS,), 0, SPECIES), jax.random.fold_in(streams_of[7], 1), 0, SPECIES - 1).astype(jnp.int32),
        "channels": place_ends((jax.random.randint(streams_of[8], (ATOMS, NPROJ), 0, 4) < 3).astype(jnp.int32), jax.random.fold_in(streams_of[8], 1), 0, 1),
        "coupling": noise(streams_of[9], (SPECIES, NPROJ, NPROJ), 2.0, 8.0, (), jnp.float32),
    }


time_step = 0.01
kinetic_scale = 0.5 * (2.0 * math.pi / 38.0) ** 2
highest = lax.Precision.HIGHEST


def signed_modes(length):
    modes = jnp.arange(length, dtype=jnp.int32)
    return jnp.where(modes < length // 2, modes, modes - length).astype(jnp.float32)


def reference(psi_real, psi_imag, potential, vector_potential, occupation, projectors, box_offsets, species, channels, coupling):
    dtype = psi_real.dtype
    shift_x = signed_modes(NX) + vector_potential[0]
    shift_y = signed_modes(NY) + vector_potential[1]
    shift_z = signed_modes(NZ) + vector_potential[2]
    kinetic = kinetic_scale * (shift_x[:, None, None] ** 2 + shift_y[None, :, None] ** 2 + shift_z[None, None, :] ** 2)

    def kinetic_one(pair):
        field = jnp.fft.fftn(pair[0] + 1j * pair[1])
        back = jnp.fft.ifftn(field * kinetic)
        return jnp.real(back).astype(dtype), jnp.imag(back).astype(dtype)

    cell = jnp.arange(BX * BY * BZ, dtype=jnp.int32)
    grid_x = (box_offsets[0][:, None] + cell // (BY * BZ)) % NX
    grid_y = (box_offsets[1][:, None] + (cell // BZ) % BY) % NY
    grid_z = (box_offsets[2][:, None] + cell % BZ) % NZ
    theta = 2.0 * math.pi * (vector_potential[0] * grid_x.astype(dtype) / NX + vector_potential[1] * grid_y.astype(dtype) / NY + vector_potential[2] * grid_z.astype(dtype) / NZ)
    cosine = jnp.cos(theta)
    sine = jnp.sin(theta)
    flat = (grid_x * NY + grid_y) * NZ + grid_z
    gates = channels.astype(dtype)
    table = coupling[species] * gates[:, :, None] * gates[:, None, :]

    def nonlocal_term(real_part, imag_part):
        orbs = real_part.shape[0]
        flat_real = real_part.reshape(orbs, -1)
        flat_imag = imag_part.reshape(orbs, -1)
        take_real = flat_real[:, flat]
        take_imag = flat_imag[:, flat]
        turned_real = cosine * take_real - sine * take_imag
        turned_imag = sine * take_real + cosine * take_imag
        coef_real = jnp.einsum("apc,oac->oap", projectors, turned_real, precision=highest)
        coef_imag = jnp.einsum("apc,oac->oap", projectors, turned_imag, precision=highest)
        dual_real = jnp.einsum("apq,oaq->oap", table, coef_real, precision=highest)
        dual_imag = jnp.einsum("apq,oaq->oap", table, coef_imag, precision=highest)
        back_real = jnp.einsum("apc,oap->oac", projectors, dual_real, precision=highest)
        back_imag = jnp.einsum("apc,oap->oac", projectors, dual_imag, precision=highest)
        placed_real = cosine * back_real + sine * back_imag
        placed_imag = cosine * back_imag - sine * back_real
        out_real = jnp.zeros_like(flat_real).at[:, flat].add(placed_real)
        out_imag = jnp.zeros_like(flat_imag).at[:, flat].add(placed_imag)
        return out_real.reshape(real_part.shape), out_imag.reshape(imag_part.shape)

    def hamiltonian(real_part, imag_part):
        kin_real, kin_imag = lax.map(kinetic_one, (real_part, imag_part))
        far_real, far_imag = nonlocal_term(real_part, imag_part)
        return kin_real + potential * real_part + far_real, kin_imag + potential * imag_part + far_imag

    first_real, first_imag = hamiltonian(psi_real, psi_imag)
    step_real = time_step * first_imag
    step_imag = -time_step * first_real
    second_real, second_imag = hamiltonian(step_real, step_imag)
    new_real = psi_real + step_real + 0.5 * time_step * second_imag
    new_imag = psi_imag + step_imag - 0.5 * time_step * second_real
    density = jnp.sum(occupation[:, None, None, None] * (new_real * new_real + new_imag * new_imag), axis=0)
    return new_real, new_imag, density
```

```python
import functools
import math

import jax
import jax.numpy as jnp
import numpy as np
from jax import lax
from jax.experimental import pallas as pl
from jax.experimental.pallas import tpu as pltpu
from jax.sharding import PartitionSpec as P

NX = 64
NY = 64
NZ = 128
BOX = 16
NPROJ = 8
SLABS = 32
BANDS = 16
REACH = 9
KINDS = 4
LANES = 128
IMAG = 64

time_step = 0.01
kinetic_scale = 0.5 * (2.0 * math.pi / 38.0) ** 2
highest = lax.Precision.HIGHEST
f32 = jnp.float32
i32 = jnp.int32


def circulant(length):
    modes = np.arange(length)
    modes = np.where(modes < length // 2, modes, modes - length).astype(np.float64)
    steps = np.arange(length)
    wave = np.exp(2j * np.pi * np.outer(steps, modes) / length) / length
    apart = (steps[:, None] - steps[None, :]) % length
    return (wave @ modes**2)[apart] * kinetic_scale, (wave @ modes)[apart] * 2.0 * kinetic_scale


def blocks(matrix):
    return np.array([[matrix.real, -matrix.imag], [matrix.imag, matrix.real]])


def along_x(matrix):
    whole = blocks(matrix).reshape(2, 2, SLABS, 2, SLABS, 2)
    out = np.einsum("cdipjq,yz->iycpjzdq", whole, np.eye(2))
    return out.reshape(256, 256).astype(np.float32)


def along_y(matrix):
    out = np.einsum("cdyz,pq->cpydqz", blocks(matrix), np.eye(2))
    return out.reshape(256, 256).astype(np.float32)


def along_z(matrix):
    return np.einsum("cdyz->dzcy", blocks(matrix)).reshape(256, 256).astype(np.float32)


def tables():
    x2, x1 = circulant(NX)
    y2, y1 = circulant(NY)
    z2, z1 = circulant(NZ)
    return (
        np.stack([along_x(x2), along_x(x1)]),
        np.stack([along_y(y2), along_y(y1)]),
        np.stack([along_z(z2), along_z(z1)]),
    )


def halves(value):
    high = value.astype(jnp.bfloat16)
    low = (value - high.astype(f32)).astype(jnp.bfloat16)
    return high, low


def dot3(left, right):
    left_high, left_low = halves(left)
    right_high, right_low = halves(right)
    dot = functools.partial(jnp.dot, preferred_element_type=f32)
    return dot(left_high, right_high) + (dot(left_high, right_low) + dot(left_low, right_high))


def group_matrix():
    row = lax.broadcasted_iota(i32, (NPROJ, LANES), 0)
    lane = lax.broadcasted_iota(i32, (NPROJ, LANES), 1)
    return (lane // BOX == row).astype(f32)


def kinetic_x(field, table_ref, shift):
    moved = dot3(table_ref[0] + shift * table_ref[1], field)
    return moved + (kinetic_scale * shift * shift) * field


def kinetic_yz(field, y_ref, z_ref, shift_y, shift_z):
    along = dot3(y_ref[0] + shift_y * y_ref[1], field)
    wide = jnp.concatenate([field[:128], field[128:]], axis=1)
    across = dot3(wide, z_ref[0] + shift_z * z_ref[1])
    across = jnp.concatenate([across[:, :128], across[:, 128:]], axis=0)
    constant = kinetic_scale * (shift_y * shift_y + shift_z * shift_z)
    return along + across + constant * field


def pack_body(index_ref, boxes_ref, species_ref, channels_ref, real_ref, imag_ref, proj_ref, out_ref, rows_ref):
    slab = index_ref[0]
    band = index_ref[1]
    out_ref[...] = jnp.zeros_like(out_ref)
    rows_ref[...] = jnp.zeros_like(rows_ref)
    for y in range(2):
        for part, ref in enumerate((real_ref, imag_ref)):
            for plane in range(2):
                row = y * 4 + part * 2 + plane
                out_ref[pl.ds(row, SLABS, stride=24), :] = ref[pl.ds(plane * NY + y, SLABS, stride=2), :]
    sub = lax.broadcasted_iota(i32, (NPROJ, LANES), 0)
    lane = lax.broadcasted_iota(i32, (NPROJ, LANES), 1)
    own = lane // BOX == sub
    pick = (band % 8) * BOX + lane % BOX
    for atom in range(4):
        for cut in range(BOX):
            start = pl.multiple_of((2 * cut + band // 8) * LANES, LANES)
            tile = proj_ref[atom, :, pl.ds(start, LANES)]
            tile = jnp.take_along_axis(tile, pick, axis=1)
            line = jnp.sum(jnp.where(own, tile, 0.0), axis=0, keepdims=True)
            rows_ref[pl.ds(atom * 24 + 1 + cut, 1), :] = line
    facts = jnp.zeros((NPROJ, LANES), f32)
    for atom in range(4):
        for channel in range(NPROJ):
            here = (sub == channel) & (lane == atom)
            facts = jnp.where(here, channels_ref[atom, channel].astype(f32), facts)
        facts = jnp.where(lane == 4 + atom, species_ref[atom].astype(f32), facts)
        facts = jnp.where(lane == 8 + atom, boxes_ref[1, atom].astype(f32), facts)
        facts = jnp.where(lane == 12 + atom, boxes_ref[2, atom].astype(f32), facts)
    for distance in range(REACH):
        target = (slab + distance) % SLABS
        for atom in range(4):
            start = 2 * distance + 1 - boxes_ref[0, atom] % 2
            out_ref[pl.ds(target * 24 + 8 + 2 * atom, 2), :] = rows_ref[pl.ds(atom * 24 + start, 2), :]
        out_ref[pl.ds(pl.multiple_of(target * 24 + 16, 8), 8), :] = facts


def pick_body(index_ref, got_ref, coupling_ref, proj_ref, table_ref, boxes_ref):
    slab = index_ref[0]
    lane = lax.broadcasted_iota(i32, (NPROJ, LANES), 1)
    zero = jnp.zeros((NPROJ, LANES), f32)
    gates, kind, first_y, first_z = zero, zero, zero, zero
    for distance in range(REACH):
        source = (slab + SLABS - distance) % SLABS
        proj_ref[pl.ds(distance * 8, 8), :] = got_ref[pl.ds(pl.multiple_of(source * 24 + 8, 8), 8), :]
        facts = got_ref[pl.ds(pl.multiple_of(source * 24 + 16, 8), 8), :]
        here = lane // 4 == distance

        def moved(offset):
            return jnp.where(here, pltpu.roll(facts, (4 * distance - offset) % LANES, 1), 0.0)

        gates += moved(0)
        kind += moved(4)
        first_y += moved(8)
        first_z += moved(12)
    gates += pltpu.roll(gates, IMAG, 1)
    kind += pltpu.roll(kind, IMAG, 1)
    for other in range(NPROJ):
        value = zero
        for which in range(KINDS):
            column = coupling_ref[which][:, other : other + 1]
            value = jnp.where(kind == float(which), column, value)
        table_ref[pl.ds(other * 8, 8), :] = value * gates * gates[other : other + 1, :]
    sub = lax.broadcasted_iota(i32, (NPROJ, LANES), 0)
    boxes_ref[...] = jnp.where(sub == 0, first_y, first_z).astype(i32)


def local_body(index_ref, vector_ref, real_ref, imag_ref, pot_ref, y_ref, z_ref, out_ref, turn_ref):
    slab = index_ref[0]
    field = jnp.concatenate([real_ref[...], imag_ref[...]], axis=0)
    out = kinetic_yz(field, y_ref, z_ref, vector_ref[1], vector_ref[2])
    pot = pot_ref[...]
    out_ref[...] = out + jnp.concatenate([pot, pot], axis=0) * field
    row = lax.broadcasted_iota(i32, (128, LANES), 0)
    x = (slab * 2 + row // NY).astype(f32)
    y = (row % NY).astype(f32)
    z = lax.broadcasted_iota(i32, (128, LANES), 1).astype(f32)
    turns = vector_ref[0] * x / NX + vector_ref[1] * y / NY + vector_ref[2] * z / NZ
    turns = turns - jnp.floor(turns + 0.5)
    theta = (2.0 * math.pi) * turns
    turn_ref[0] = jnp.cos(theta)
    turn_ref[1] = jnp.sin(theta)


def columns_body(width, vector_ref, got_ref, x_ref, out_ref):
    field = got_ref[:, 0:8, :].reshape(256, LANES)
    out_ref[...] = kinetic_x(field, x_ref, vector_ref[0])


def project(boxes_ref, proj_ref, real, imag, turn_ref, field_ref, sums_ref):
    cosine, sine = turn_ref[0], turn_ref[1]
    turned = (cosine * real - sine * imag, sine * real + cosine * imag)
    for part in range(2):
        for plane in range(2):
            base = (part * 2 + plane) * 80
            field_ref[pl.ds(base, 64), :] = turned[part][plane * 64 : plane * 64 + 64]
            field_ref[pl.ds(base + 64, 16), :] = turned[part][plane * 64 : plane * 64 + 16]
    sums_ref[...] = jnp.zeros_like(sums_ref)
    lane = lax.broadcasted_iota(i32, (BOX, LANES), 1)

    def one(atom, carry):
        first_y = boxes_ref[0, atom]
        first_z = boxes_ref[1, atom]
        pick = (first_z + lane % BOX) % LANES
        total = [None, None]
        for plane in range(2):
            beta = proj_ref[pl.ds(atom * 2 + plane, BOX, stride=72), :]
            for part in range(2):
                rows = field_ref[pl.ds((part * 2 + plane) * 80 + first_y, BOX), :]
                term = beta * jnp.take_along_axis(rows, pick, axis=1)
                total[part] = term if plane == 0 else total[part] + term
        for part in range(2):
            sums_ref[pl.ds(part * IMAG + atom, 1), :] = jnp.sum(total[part], axis=0, keepdims=True)
        return carry

    lax.fori_loop(0, 4 * REACH, one, 0, unroll=4)
    return lax.dot_general(
        group_matrix(), sums_ref[...], (((1,), (1,)), ((), ())), precision=highest, preferred_element_type=f32
    )


def spread(slab, boxes_ref, proj_ref, table_ref, got_ref, width, turn_ref, place_ref, dual_ref):
    lane = lax.broadcasted_iota(i32, (NPROJ, LANES), 1)
    box = (lane % IMAG) // 4
    coef = jnp.zeros((NPROJ, LANES), f32)
    for offset in range(1 - REACH, REACH):
        source = (slab + SLABS + offset) % SLABS
        share = got_ref[source, width - 8 : width, :]
        if offset != 0:
            share = pltpu.roll(share, (-4 * offset) % LANES, 1)
        sent = box + offset
        coef += jnp.where((box < REACH) & (sent >= 0) & (sent < REACH), share, 0.0)
    dual = jnp.zeros((NPROJ, LANES), f32)
    for other in range(NPROJ):
        dual += table_ref[pl.ds(other * 8, 8), :] * coef[other : other + 1, :]
    dual_ref[...] = lax.dot_general(
        dual, group_matrix(), (((0,), (0,)), ((), ())), precision=highest, preferred_element_type=f32
    )
    place_ref[...] = jnp.zeros_like(place_ref)
    wide = lax.broadcasted_iota(i32, (BOX, LANES), 1)

    def one(atom, carry):
        first_y = boxes_ref[0, atom]
        first_z = boxes_ref[1, atom]
        inside = (wide + LANES - first_z) % LANES < BOX
        for plane in range(2):
            beta = proj_ref[pl.ds(atom * 2 + plane, BOX, stride=72), :]
            for part in range(2):
                value = beta * dual_ref[pl.ds(part * IMAG + atom, 1), :]
                value += pltpu.roll(value, 64, 1)
                value += pltpu.roll(value, 32, 1)
                value += pltpu.roll(value, 16, 1)
                value = jnp.where(inside, pltpu.roll(value, first_z, 1), 0.0)
                place_ref[pl.ds((part * 2 + plane) * 80 + first_y, BOX), :] += value
        return carry

    lax.fori_loop(0, 4 * REACH, one, 0, unroll=2)
    for block in range(4):
        place_ref[pl.ds(block * 80, 16), :] += place_ref[pl.ds(block * 80 + 64, 16), :]
    back_real = jnp.concatenate([place_ref[pl.ds(0, 64), :], place_ref[pl.ds(80, 64), :]], axis=0)
    back_imag = jnp.concatenate([place_ref[pl.ds(160, 64), :], place_ref[pl.ds(240, 64), :]], axis=0)
    cosine, sine = turn_ref[0], turn_ref[1]
    return cosine * back_real + sine * back_imag, cosine * back_imag - sine * back_real


def unpack(got_ref, width, field_ref):
    for y in range(2):
        for part in range(2):
            for plane in range(2):
                row = y * 4 + part * 2 + plane
                start = part * 128 + plane * 64 + y
                field_ref[pl.ds(start, SLABS, stride=2), :] = got_ref[:, row, :]


def coef_body(boxes_ref, proj_ref, real_ref, imag_ref, turn_ref, moved_ref, out_ref, field_ref, sums_ref):
    coef = project(boxes_ref, proj_ref, real_ref[...], imag_ref[...], turn_ref, field_ref, sums_ref)
    out_ref[:, 0:8, :] = moved_ref[...].reshape(SLABS, 8, LANES)
    out_ref[:, 8:16, :] = jnp.broadcast_to(coef[None], (SLABS, 8, LANES))


def first_body(
    index_ref, boxes_ref, proj_ref, table_ref, got_ref, turn_ref, local_ref,
    first_ref, out_ref, field_ref, sums_ref, place_ref, dual_ref,
):
    slab = index_ref[0]
    unpack(got_ref, 16, first_ref)
    far_real, far_imag = spread(
        slab, boxes_ref, proj_ref, table_ref, got_ref, 16, turn_ref, place_ref, dual_ref
    )
    real = first_ref[0:128, :] + local_ref[0:128, :] + far_real
    imag = first_ref[128:256, :] + local_ref[128:256, :] + far_imag
    first_ref[0:128, :] = real
    first_ref[128:256, :] = imag
    for y in range(2):
        for part in range(2):
            for plane in range(2):
                row = y * 4 + part * 2 + plane
                start = part * 128 + plane * 64 + y
                out_ref[:, row, :] = first_ref[pl.ds(start, SLABS, stride=2), :]
    coef = project(boxes_ref, proj_ref, real, imag, turn_ref, field_ref, sums_ref)
    out_ref[:, 8:16, :] = jnp.broadcast_to(coef[None], (SLABS, 8, LANES))


def second_body(
    index_ref, vector_ref, boxes_ref, proj_ref, table_ref, got_ref, turn_ref, first_ref, pot_ref, y_ref, z_ref,
    out_ref, place_ref, dual_ref,
):
    slab = index_ref[0]
    field = first_ref[...]
    near = kinetic_yz(field, y_ref, z_ref, vector_ref[1], vector_ref[2])
    far_real, far_imag = spread(
        slab, boxes_ref, proj_ref, table_ref, got_ref, 16, turn_ref, place_ref, dual_ref
    )
    pot = pot_ref[...]
    out_ref[0:128, :] = near[:128] + pot * field[:128] + far_real
    out_ref[128:256, :] = near[128:] + pot * field[128:] + far_imag


def final_body(occupation_ref, real_ref, imag_ref, first_ref, near_ref, got_ref, new_real_ref, new_imag_ref, out_ref, field_ref):
    unpack(got_ref, 8, field_ref)
    half = 0.5 * time_step * time_step
    new_real = real_ref[...] + time_step * first_ref[128:256, :] - half * (near_ref[0:128, :] + field_ref[0:128, :])
    new_imag = imag_ref[...] - time_step * first_ref[0:128, :] - half * (near_ref[128:256, :] + field_ref[128:256, :])
    new_real_ref[...] = new_real
    new_imag_ref[...] = new_imag
    weighted = occupation_ref[0] * (new_real * new_real + new_imag * new_imag)
    weighted = weighted.reshape(2, BANDS, 4, LANES)
    for plane in range(2):
        out_ref[:, pl.ds(plane * 4, 4), :] = weighted[plane]


def smem():
    return pl.BlockSpec(memory_space=pltpu.SMEM)


def vmem():
    return pl.BlockSpec(memory_space=pltpu.VMEM)


def call(body, scalars, arrays, outs, scratch=()):
    several = isinstance(outs, tuple)
    return pl.pallas_call(
        body,
        out_shape=outs,
        in_specs=[smem()] * len(scalars) + [vmem()] * len(arrays),
        out_specs=tuple(vmem() for _ in outs) if several else vmem(),
        scratch_shapes=list(scratch),
        compiler_params=pltpu.CompilerParams(vmem_limit_bytes=24 * 1024 * 1024),
    )(*scalars, *arrays)


def shape(*dims, dtype=f32):
    return jax.ShapeDtypeStruct(dims, dtype)


def exchange(value, axis):
    return lax.all_to_all(value, axis, split_axis=0, concat_axis=0, tiled=True)


def per_device(
    psi_real, psi_imag, potential, vector_potential, occupation, projectors, box_offsets, species, channels, coupling
):
    x_table, y_table, z_table = (jnp.asarray(table) for table in tables())
    index = jnp.stack([lax.axis_index("fft"), lax.axis_index("band")]).astype(i32)
    real = psi_real.reshape(128, LANES)
    imag = psi_imag.reshape(128, LANES)
    pot = potential.reshape(128, LANES)

    packed = call(
        pack_body, (index, box_offsets, species, channels), (real, imag, projectors),
        shape(SLABS * 24, LANES), (pltpu.VMEM((96, LANES), f32),),
    )
    got = exchange(packed.reshape(SLABS, 24, LANES), "fft")
    local, turn = call(
        local_body, (index, vector_potential), (real, imag, pot, y_table, z_table),
        (shape(256, LANES), shape(2, 128, LANES)),
    )
    picked, table, boxes = call(
        pick_body, (index,), (got.reshape(SLABS * 24, LANES), coupling),
        (shape(72, LANES), shape(64, LANES), shape(8, LANES, dtype=i32)),
    )
    beta = lax.all_gather(picked, "band").reshape(BANDS * 72, LANES)
    moved = call(
        functools.partial(columns_body, 24), (vector_potential,), (got, x_table), shape(256, LANES)
    )
    window = pltpu.VMEM((320, LANES), f32)
    square = pltpu.VMEM((128, LANES), f32)
    shares = call(
        coef_body, (boxes,), (beta, real, imag, turn, moved), shape(SLABS, 16, LANES), (window, square)
    )
    got = exchange(shares, "fft")
    first, shares = call(
        first_body, (index, boxes), (beta, table, got, turn, local),
        (shape(256, LANES), shape(SLABS, 16, LANES)), (window, square, window, square),
    )
    got = exchange(shares, "fft")
    moved = call(
        functools.partial(columns_body, 16), (vector_potential,), (got, x_table), shape(256, LANES)
    )
    back = exchange(moved.reshape(SLABS, 8, LANES), "fft")
    near = call(
        second_body, (index, vector_potential, boxes),
        (beta, table, got, turn, first, pot, y_table, z_table), shape(256, LANES), (window, square),
    )
    new_real, new_imag, weighted = call(
        final_body, (occupation,), (real, imag, first, near, back),
        (shape(128, LANES), shape(128, LANES), shape(BANDS, 8, LANES)), (pltpu.VMEM((256, LANES), f32),),
    )
    density = jnp.sum(exchange(weighted, "band"), axis=0).reshape(2, 4, LANES)
    whole = (1, 2, NY, NZ)
    return new_real.reshape(whole), new_imag.reshape(whole), density


def solution(mesh):
    placed = (
        P("band", "fft", None, None),
        P("band", "fft", None, None),
        P("fft", None, None),
        P(),
        P("band"),
        P("fft", None, None),
        P(None, "fft"),
        P("fft"),
        P("fft", None),
        P(),
    )
    return jax.shard_map(
        per_device,
        mesh=mesh,
        in_specs=placed,
        out_specs=(
            P("band", "fft", None, None),
            P("band", "fft", None, None),
            P("fft", "band", None),
        ),
        check_vma=False,
    )
```

```python
import functools
import math

import jax
import jax.numpy as jnp
import numpy as np
from jax import lax
from jax.experimental import pallas as pl
from jax.experimental.pallas import tpu as pltpu
from jax.sharding import PartitionSpec as P

NX = 64
NY = 64
NZ = 128
BOX = 16
NPROJ = 8
SLABS = 32
BANDS = 16
REACH = 9
KINDS = 4
LANES = 128
IMAG = 64

time_step = 0.01
kinetic_scale = 0.5 * (2.0 * math.pi / 38.0) ** 2
highest = lax.Precision.HIGHEST
f32 = jnp.float32
i32 = jnp.int32


def circulant(length):
    modes = np.arange(length)
    modes = np.where(modes < length // 2, modes, modes - length).astype(np.float64)
    steps = np.arange(length)
    wave = np.exp(2j * np.pi * np.outer(steps, modes) / length) / length
    apart = (steps[:, None] - steps[None, :]) % length
    return (wave @ modes**2)[apart] * kinetic_scale, (wave @ modes)[apart] * 2.0 * kinetic_scale


def blocks(matrix):
    return np.array([[matrix.real, -matrix.imag], [matrix.imag, matrix.real]])


def along_x(matrix):
    whole = blocks(matrix).reshape(2, 2, SLABS, 2, SLABS, 2)
    out = np.einsum("cdipjq,yz->iycpjzdq", whole, np.eye(2))
    return out.reshape(256, 256).astype(np.float32)


def along_y(matrix):
    out = np.einsum("cdyz,pq->cpydqz", blocks(matrix), np.eye(2))
    return out.reshape(256, 256).astype(np.float32)


def along_z(matrix):
    return np.einsum("cdyz->dzcy", blocks(matrix)).reshape(256, 256).astype(np.float32)


def tables():
    x2, x1 = circulant(NX)
    y2, y1 = circulant(NY)
    z2, z1 = circulant(NZ)
    return (
        np.stack([along_x(x2), along_x(x1)]),
        np.stack([along_y(y2), along_y(y1)]),
        np.stack([along_z(z2), along_z(z1)]),
    )


def halves(value):
    high = value.astype(jnp.bfloat16)
    low = (value - high.astype(f32)).astype(jnp.bfloat16)
    return high, low


def dot3(left, right):
    left_high, left_low = halves(left)
    right_high, right_low = halves(right)
    dot = functools.partial(jnp.dot, preferred_element_type=f32)
    return dot(left_high, right_high) + (dot(left_high, right_low) + dot(left_low, right_high))


def group_matrix():
    row = lax.broadcasted_iota(i32, (NPROJ, LANES), 0)
    lane = lax.broadcasted_iota(i32, (NPROJ, LANES), 1)
    return (lane // BOX == row).astype(f32)


def kinetic_yz(field, y_ref, z_ref, shift_y, shift_z):
    along = dot3(y_ref[0] + shift_y * y_ref[1], field)
    wide = jnp.concatenate([field[:128], field[128:]], axis=1)
    across = dot3(wide, z_ref[0] + shift_z * z_ref[1])
    across = jnp.concatenate([across[:, :128], across[:, 128:]], axis=0)
    constant = kinetic_scale * (shift_y * shift_y + shift_z * shift_z)
    return along + across + constant * field


def kinetic_x(field, high_ref, low_ref, shift):
    field_high, field_low = halves(field)
    dot = functools.partial(jnp.dot, preferred_element_type=f32)
    high = high_ref[...]
    moved = dot(high, field_high) + (dot(high, field_low) + dot(low_ref[...], field_high))
    return moved + (kinetic_scale * shift * shift) * field


def pack_body(index_ref, boxes_ref, species_ref, channels_ref, proj_ref, own_ref, near_ref, rows_ref):
    core = index_ref[1] % 2
    sub = lax.broadcasted_iota(i32, (NPROJ, LANES), 0)
    lane = lax.broadcasted_iota(i32, (NPROJ, LANES), 1)
    cell = lane % BOX
    group = lane // BOX
    skew = (group + sub) % 8 * BOX + cell
    shift = (sub - group) % 8
    rows_ref[...] = jnp.zeros_like(rows_ref)
    for atom in range(4):
        last = shift * BOX + (cell + 256 - boxes_ref[2, atom]) % BOX
        for cut in range(BOX):
            start = pl.multiple_of((2 * cut + core) * LANES, LANES)
            tile = proj_ref[atom, :, pl.ds(start, LANES)]
            tile = jnp.take_along_axis(tile, skew, axis=1)
            tile = jnp.take_along_axis(tile, shift, axis=0)
            tile = jnp.take_along_axis(tile, last, axis=1)
            rows_ref[pl.ds(atom * 160 + 8 + cut * 8, 8), :] = tile
    facts = jnp.zeros((NPROJ, LANES), f32)
    for atom in range(4):
        for channel in range(NPROJ):
            here = (sub == channel) & (lane == atom)
            facts = jnp.where(here, channels_ref[atom, channel].astype(f32), facts)
        facts = jnp.where(lane == 4 + atom, species_ref[atom].astype(f32), facts)
        facts = jnp.where(lane == 8 + atom, boxes_ref[1, atom].astype(f32), facts)
        facts = jnp.where(lane == 12 + atom, boxes_ref[2, atom].astype(f32), facts)
    for atom in range(4):
        odd = boxes_ref[0, atom] % 2
        for distance in range(REACH):
            start = pl.multiple_of(atom * 160 + (2 * distance + 1 - odd) * 8, 8)
            piece = rows_ref[pl.ds(start, 16), :]
            if distance == 0:
                near_ref[pl.ds(atom * 16, 16), :] = piece
            else:
                own_ref[pl.ds((distance - 1) * 64 + atom * 16, 16), :] = piece
    own_ref[pl.ds(512, 8), :] = facts


def route_body(index_ref, own_ref, near_ref, passed_ref, out_ref, last_ref):
    place = index_ref[0] % 8
    for target in range(8):

        @pl.when(target == place)
        def _():
            out_ref[target, 0:64, :] = near_ref[...]
            out_ref[target, 64:72, :] = own_ref[512:520, :]

        @pl.when(target > place)
        def _():
            start = pl.multiple_of((target - place - 1) * 64, 64)
            out_ref[target, 0:64, :] = own_ref[pl.ds(start, 64), :]
            out_ref[target, 64:72, :] = own_ref[512:520, :]

        @pl.when(target < place)
        def _():
            start = pl.multiple_of((target - place + 7) * 64, 64)
            out_ref[target, 0:64, :] = passed_ref[pl.ds(start, 64), :]
            out_ref[target, 64:72, :] = passed_ref[512:520, :]

    last_ref[...] = passed_ref[448:520, :]


def pick_body(index_ref, got_ref, last_ref, coupling_ref, proj_ref, table_ref, boxes_ref):
    place = index_ref[0] % 8
    lane = lax.broadcasted_iota(i32, (NPROJ, LANES), 1)
    zero = jnp.zeros((NPROJ, LANES), f32)
    gates, kind, first_y, first_z = zero, zero, zero, zero
    for distance in range(REACH):
        if distance < 8:
            source = (place + 8 - distance) % 8
            proj_ref[pl.ds(distance * 64, 64), :] = got_ref[source, 0:64, :]
            facts = got_ref[source, 64:72, :]
        else:
            proj_ref[pl.ds(distance * 64, 64), :] = last_ref[0:64, :]
            facts = last_ref[64:72, :]
        here = lane // 4 == distance

        def moved(offset):
            return jnp.where(here, pltpu.roll(facts, (4 * distance - offset) % LANES, 1), 0.0)

        gates += moved(0)
        kind += moved(4)
        first_y += moved(8)
        first_z += moved(12)
    gates += pltpu.roll(gates, IMAG, 1)
    kind += pltpu.roll(kind, IMAG, 1)
    for other in range(NPROJ):
        value = zero
        for which in range(KINDS):
            column = coupling_ref[which][:, other : other + 1]
            value = jnp.where(kind == float(which), column, value)
        table_ref[pl.ds(other * 8, 8), :] = value * gates * gates[other : other + 1, :]
    sub = lax.broadcasted_iota(i32, (NPROJ, LANES), 0)
    boxes_ref[...] = jnp.where(sub == 0, first_y, first_z).astype(i32)


def local_body(
    index_ref, vector_ref, real_ref, imag_ref, pot_ref, x_ref, y_ref, z_ref, out_ref, turn_ref, high_ref, low_ref
):
    slab = index_ref[0]
    field = jnp.concatenate([real_ref[...], imag_ref[...]], axis=0)
    out = kinetic_yz(field, y_ref, z_ref, vector_ref[1], vector_ref[2])
    pot = pot_ref[...]
    out_ref[...] = out + jnp.concatenate([pot, pot], axis=0) * field
    row = lax.broadcasted_iota(i32, (128, LANES), 0)
    x = (slab * 2 + row // NY).astype(f32)
    y = (row % NY).astype(f32)
    z = lax.broadcasted_iota(i32, (128, LANES), 1).astype(f32)
    turns = vector_ref[0] * x / NX + vector_ref[1] * y / NY + vector_ref[2] * z / NZ
    turns = turns - jnp.floor(turns + 0.5)
    theta = (2.0 * math.pi) * turns
    turn_ref[0] = jnp.cos(theta)
    turn_ref[1] = jnp.sin(theta)
    high, low = halves(x_ref[0] + vector_ref[0] * x_ref[1])
    high_ref[...] = high
    low_ref[...] = low


def project(boxes_ref, proj_ref, real, imag, turn_ref, field_ref, sums_ref):
    cosine, sine = turn_ref[0], turn_ref[1]
    turned = (cosine * real - sine * imag, sine * real + cosine * imag)
    for part in range(2):
        for plane in range(2):
            base = (part * 2 + plane) * 80
            field_ref[pl.ds(base, 64), :] = turned[part][plane * 64 : plane * 64 + 64]
            field_ref[pl.ds(base + 64, 16), :] = turned[part][plane * 64 : plane * 64 + 16]
    sums_ref[...] = jnp.zeros_like(sums_ref)
    cell = lax.broadcasted_iota(i32, (BOX, LANES), 1) % BOX

    def one(atom, carry):
        first_y = boxes_ref[0, atom]
        first_z = boxes_ref[1, atom]
        pick = (first_z + (cell + LANES - first_z) % BOX) % LANES
        total = [None, None]
        for plane in range(2):
            start = pl.multiple_of(atom * 16 + plane * 8, 8)
            beta = jnp.concatenate([proj_ref[0, pl.ds(start, 8), :], proj_ref[1, pl.ds(start, 8), :]], axis=0)
            for part in range(2):
                rows = field_ref[pl.ds((part * 2 + plane) * 80 + first_y, BOX), :]
                term = beta * jnp.take_along_axis(rows, pick, axis=1)
                total[part] = term if plane == 0 else total[part] + term
        for part in range(2):
            sums_ref[pl.ds(part * IMAG + atom, 1), :] = jnp.sum(total[part], axis=0, keepdims=True)
        return carry

    lax.fori_loop(0, 4 * REACH, one, 0, unroll=4)
    return lax.dot_general(
        group_matrix(), sums_ref[...], (((1,), (1,)), ((), ())), precision=highest, preferred_element_type=f32
    )


def spread(slab, boxes_ref, proj_ref, table_ref, got_ref, turn_ref, place_ref, dual_ref):
    lane = lax.broadcasted_iota(i32, (NPROJ, LANES), 1)
    box = (lane % IMAG) // 4
    coef = jnp.zeros((NPROJ, LANES), f32)
    for offset in range(1 - REACH, REACH):
        source = (slab + SLABS + offset) % SLABS
        share = got_ref[source, 8:16, :]
        if offset != 0:
            share = pltpu.roll(share, (-4 * offset) % LANES, 1)
        sent = box + offset
        coef += jnp.where((box < REACH) & (sent >= 0) & (sent < REACH), share, 0.0)
    dual = jnp.zeros((NPROJ, LANES), f32)
    for other in range(NPROJ):
        dual += table_ref[pl.ds(other * 8, 8), :] * coef[other : other + 1, :]
    dual_ref[...] = lax.dot_general(
        dual, group_matrix(), (((0,), (0,)), ((), ())), precision=highest, preferred_element_type=f32
    )
    place_ref[...] = jnp.zeros_like(place_ref)
    left = lax.broadcasted_iota(i32, (256, 256), 0)
    right = lax.broadcasted_iota(i32, (256, 256), 1)
    gather = ((left // LANES == right // LANES) & (left % BOX == right % BOX)).astype(f32).astype(jnp.bfloat16)
    wide = lax.broadcasted_iota(i32, (8, 2 * LANES), 1) % LANES
    dot = functools.partial(jnp.dot, preferred_element_type=f32)
    for distance in range(REACH):
        rows = []
        for half in range(2):
            for atom in range(4 * distance, 4 * distance + 4):
                beta = proj_ref[half, pl.ds(atom * 16, 16), :]
                real = beta * dual_ref[pl.ds(atom, 1), :]
                imag = beta * dual_ref[pl.ds(IMAG + atom, 1), :]
                rows.append(jnp.concatenate([real, imag], axis=1))
        high, low = halves(jnp.concatenate(rows, axis=0))
        value = dot(high, gather) + dot(low, gather)
        for atom in range(4 * distance, 4 * distance + 4):
            first_y = boxes_ref[0, atom]
            first_z = boxes_ref[1, atom]
            inside = (wide + LANES - first_z) % LANES < BOX
            for plane in range(2):
                parts = []
                for half in range(2):
                    start = half * 64 + (atom % 4) * 16 + plane * 8
                    parts.append(jnp.where(inside, value[start : start + 8], 0.0))
                both = jnp.concatenate(parts, axis=0)
                place_ref[pl.ds(plane * 80 + first_y, BOX), :] += both[:, :LANES]
                place_ref[pl.ds(160 + plane * 80 + first_y, BOX), :] += both[:, LANES:]
    for block in range(4):
        place_ref[pl.ds(block * 80, 16), :] += place_ref[pl.ds(block * 80 + 64, 16), :]
    back_real = jnp.concatenate([place_ref[pl.ds(0, 64), :], place_ref[pl.ds(80, 64), :]], axis=0)
    back_imag = jnp.concatenate([place_ref[pl.ds(160, 64), :], place_ref[pl.ds(240, 64), :]], axis=0)
    cosine, sine = turn_ref[0], turn_ref[1]
    return cosine * back_real + sine * back_imag, cosine * back_imag - sine * back_real


def columns(field_ref, out_ref):
    for y in range(2):
        for part in range(2):
            for plane in range(2):
                row = y * 4 + part * 2 + plane
                start = part * 128 + plane * 64 + y
                out_ref[:, row, :] = field_ref[pl.ds(start, SLABS, stride=2), :]


def unpack(got_ref, first_row, field_ref):
    for y in range(2):
        for part in range(2):
            for plane in range(2):
                row = y * 4 + part * 2 + plane
                start = part * 128 + plane * 64 + y
                field_ref[pl.ds(start, SLABS, stride=2), :] = got_ref[:, first_row + row, :]


def coef_body(boxes_ref, proj_ref, real_ref, imag_ref, turn_ref, out_ref, whole_ref, field_ref, sums_ref):
    real, imag = real_ref[...], imag_ref[...]
    whole_ref[0:128, :] = real
    whole_ref[128:256, :] = imag
    columns(whole_ref, out_ref)
    coef = project(boxes_ref, proj_ref, real, imag, turn_ref, field_ref, sums_ref)
    out_ref[:, 8:16, :] = jnp.broadcast_to(coef[None], (SLABS, 8, LANES))


def rest_body(
    index_ref, vector_ref, boxes_ref, proj_ref, table_ref, got_ref, turn_ref, local_ref, high_ref, low_ref,
    rest_ref, moved_ref, out_ref, place_ref, dual_ref,
):
    field = got_ref[:, 0:8, :].reshape(256, LANES)
    moved = kinetic_x(field, high_ref, low_ref, vector_ref[0])
    moved_ref[...] = moved
    out_ref[:, 8:16, :] = moved.reshape(SLABS, 8, LANES)
    far_real, far_imag = spread(
        index_ref[0], boxes_ref, proj_ref, table_ref, got_ref, turn_ref, place_ref, dual_ref
    )
    rest_ref[0:128, :] = local_ref[0:128, :] + far_real
    rest_ref[128:256, :] = local_ref[128:256, :] + far_imag
    columns(rest_ref, out_ref)


def first_body(
    vector_ref, boxes_ref, proj_ref, got_ref, turn_ref, rest_ref, moved_ref, high_ref, low_ref,
    first_ref, out_ref, field_ref, sums_ref,
):
    field = got_ref[:, 0:8, :].reshape(256, LANES) + moved_ref[...]
    out_ref[:, 0:8, :] = kinetic_x(field, high_ref, low_ref, vector_ref[0]).reshape(SLABS, 8, LANES)
    unpack(got_ref, 8, first_ref)
    real = first_ref[0:128, :] + rest_ref[0:128, :]
    imag = first_ref[128:256, :] + rest_ref[128:256, :]
    first_ref[0:128, :] = real
    first_ref[128:256, :] = imag
    coef = project(boxes_ref, proj_ref, real, imag, turn_ref, field_ref, sums_ref)
    out_ref[:, 8:16, :] = jnp.broadcast_to(coef[None], (SLABS, 8, LANES))


def second_body(vector_ref, first_ref, pot_ref, y_ref, z_ref, out_ref):
    field = first_ref[...]
    pot = pot_ref[...]
    near = kinetic_yz(field, y_ref, z_ref, vector_ref[1], vector_ref[2])
    out_ref[...] = near + jnp.concatenate([pot, pot], axis=0) * field


def final_body(
    index_ref, occupation_ref, boxes_ref, proj_ref, table_ref, got_ref, turn_ref, real_ref, imag_ref, first_ref,
    near_ref, new_real_ref, new_imag_ref, out_ref, field_ref, place_ref, dual_ref,
):
    unpack(got_ref, 0, field_ref)
    far_real, far_imag = spread(
        index_ref[0], boxes_ref, proj_ref, table_ref, got_ref, turn_ref, place_ref, dual_ref
    )
    half = 0.5 * time_step * time_step
    second_real = near_ref[0:128, :] + field_ref[0:128, :] + far_real
    second_imag = near_ref[128:256, :] + field_ref[128:256, :] + far_imag
    new_real = real_ref[...] + time_step * first_ref[128:256, :] - half * second_real
    new_imag = imag_ref[...] - time_step * first_ref[0:128, :] - half * second_imag
    new_real_ref[...] = new_real
    new_imag_ref[...] = new_imag
    weighted = occupation_ref[0] * (new_real * new_real + new_imag * new_imag)
    weighted = weighted.reshape(2, BANDS, 4, LANES)
    for plane in range(2):
        out_ref[:, pl.ds(plane * 4, 4), :] = weighted[plane]


def smem():
    return pl.BlockSpec(memory_space=pltpu.SMEM)


def vmem():
    return pl.BlockSpec(memory_space=pltpu.VMEM)


def call(body, scalars, arrays, outs, scratch=()):
    several = isinstance(outs, tuple)
    return pl.pallas_call(
        body,
        out_shape=outs,
        in_specs=[smem()] * len(scalars) + [vmem()] * len(arrays),
        out_specs=tuple(vmem() for _ in outs) if several else vmem(),
        scratch_shapes=list(scratch),
        compiler_params=pltpu.CompilerParams(vmem_limit_bytes=24 * 1024 * 1024),
    )(*scalars, *arrays)


def shape(*dims, dtype=f32):
    return jax.ShapeDtypeStruct(dims, dtype)


def exchange(value, axis):
    return lax.all_to_all(value, axis, split_axis=0, concat_axis=0, tiled=True)


def per_device(
    psi_real, psi_imag, potential, vector_potential, occupation, projectors, box_offsets, species, channels, coupling
):
    x_table, y_table, z_table = (jnp.asarray(table) for table in tables())
    index = jnp.stack([lax.axis_index("fft"), lax.axis_index("band")]).astype(i32)
    real = psi_real.reshape(128, LANES)
    imag = psi_imag.reshape(128, LANES)
    pot = potential.reshape(128, LANES)
    matrix = jax.ShapeDtypeStruct((256, 256), jnp.bfloat16)
    window = pltpu.VMEM((320, LANES), f32)
    square = pltpu.VMEM((128, LANES), f32)
    whole = pltpu.VMEM((256, LANES), f32)

    own, near = call(
        pack_body, (index, box_offsets, species, channels), (projectors,),
        (shape(520, LANES), shape(64, LANES)), (pltpu.VMEM((640, LANES), f32),),
    )
    passed = lax.ppermute(own, "fft", [(i, (i + 8) % SLABS) for i in range(SLABS)])
    local, turn, high, low = call(
        local_body, (index, vector_potential), (real, imag, pot, x_table, y_table, z_table),
        (shape(256, LANES), shape(2, 128, LANES), matrix, matrix),
    )
    slices, last = call(
        route_body, (index,), (own, near, passed), (shape(8, 72, LANES), shape(72, LANES))
    )
    rows = [list(range(8 * x, 8 * x + 8)) for x in range(4)]
    got = lax.all_to_all(slices, "fft", split_axis=0, concat_axis=0, tiled=True, axis_index_groups=rows)
    picked, table, boxes = call(
        pick_body, (index,), (got, last, coupling),
        (shape(576, LANES), shape(64, LANES), shape(8, LANES, dtype=i32)),
    )
    chips = [[2 * y, 2 * y + 1] for y in range(8)]
    beta = lax.all_gather(picked, "band", axis_index_groups=chips)
    shares = call(
        coef_body, (boxes,), (beta, real, imag, turn), shape(SLABS, 16, LANES), (whole, window, square)
    )
    got = exchange(shares, "fft")
    rest, moved, shares = call(
        rest_body, (index, vector_potential, boxes), (beta, table, got, turn, local, high, low),
        (shape(256, LANES), shape(256, LANES), shape(SLABS, 16, LANES)), (window, square),
    )
    got = exchange(shares, "fft")
    first, shares = call(
        first_body, (vector_potential, boxes), (beta, got, turn, rest, moved, high, low),
        (shape(256, LANES), shape(SLABS, 16, LANES)), (window, square),
    )
    got = exchange(shares, "fft")
    near = call(second_body, (vector_potential,), (first, pot, y_table, z_table), shape(256, LANES))
    new_real, new_imag, weighted = call(
        final_body, (index, occupation, boxes), (beta, table, got, turn, real, imag, first, near),
        (shape(128, LANES), shape(128, LANES), shape(BANDS, 8, LANES)), (whole, window, square),
    )
    density = jnp.sum(exchange(weighted, "band"), axis=0).reshape(2, 4, LANES)
    grid = (1, 2, NY, NZ)
    return new_real.reshape(grid), new_imag.reshape(grid), density


def solution(mesh):
    placed = (
        P("band", "fft", None, None),
        P("band", "fft", None, None),
        P("fft", None, None),
        P(),
        P("band"),
        P("fft", None, None),
        P(None, "fft"),
        P("fft"),
        P("fft", None),
        P(),
    )
    return jax.shard_map(
        per_device,
        mesh=mesh,
        in_specs=placed,
        out_specs=(
            P("band", "fft", None, None),
            P("band", "fft", None, None),
            P("fft", "band", None),
        ),
        check_vma=False,
    )
```

```python
import functools
import math

import jax
import jax.numpy as jnp
import numpy as np
from jax import lax
from jax.experimental import pallas as pl
from jax.experimental.pallas import tpu as pltpu
from jax.sharding import PartitionSpec as P

NX = 64
NY = 64
NZ = 128
BOX = 16
NPROJ = 8
SLABS = 32
BANDS = 16
REACH = 9
KINDS = 4
LANES = 128
IMAG = 64

time_step = 0.01
kinetic_scale = 0.5 * (2.0 * math.pi / 38.0) ** 2
highest = lax.Precision.HIGHEST
f32 = jnp.float32
i32 = jnp.int32


def circulant(length):
    modes = np.arange(length)
    modes = np.where(modes < length // 2, modes, modes - length).astype(np.float64)
    steps = np.arange(length)
    wave = np.exp(2j * np.pi * np.outer(steps, modes) / length) / length
    apart = (steps[:, None] - steps[None, :]) % length
    return (wave @ modes**2)[apart] * kinetic_scale, (wave @ modes)[apart] * 2.0 * kinetic_scale


def blocks(matrix):
    return np.array([[matrix.real, -matrix.imag], [matrix.imag, matrix.real]])


def along_x(matrix):
    whole = blocks(matrix).reshape(2, 2, SLABS, 2, SLABS, 2)
    out = np.einsum("cdipjq,yz->iycpjzdq", whole, np.eye(2))
    return out.reshape(256, 256).astype(np.float32)


def along_y(matrix):
    out = np.einsum("cdyz,pq->cpydqz", blocks(matrix), np.eye(2))
    return out.reshape(256, 256).astype(np.float32)


def along_z(matrix):
    return np.einsum("cdyz->dzcy", blocks(matrix)).reshape(256, 256).astype(np.float32)


def tables():
    x2, x1 = circulant(NX)
    y2, y1 = circulant(NY)
    z2, z1 = circulant(NZ)
    return (
        np.stack([along_x(x2), along_x(x1)]),
        np.stack([along_y(y2), along_y(y1)]),
        np.stack([along_z(z2), along_z(z1)]),
    )


def halves(value):
    high = value.astype(jnp.bfloat16)
    low = (value - high.astype(f32)).astype(jnp.bfloat16)
    return high, low


def dot3(left, right):
    left_high, left_low = halves(left)
    right_high, right_low = halves(right)
    dot = functools.partial(jnp.dot, preferred_element_type=f32)
    return dot(left_high, right_high) + (dot(left_high, right_low) + dot(left_low, right_high))


def group_matrix():
    row = lax.broadcasted_iota(i32, (NPROJ, LANES), 0)
    lane = lax.broadcasted_iota(i32, (NPROJ, LANES), 1)
    return (lane // BOX == row).astype(f32)


def kinetic_yz(field, y_ref, z_ref, shift_y, shift_z):
    along = dot3(y_ref[0] + shift_y * y_ref[1], field)
    wide = jnp.concatenate([field[:128], field[128:]], axis=1)
    across = dot3(wide, z_ref[0] + shift_z * z_ref[1])
    across = jnp.concatenate([across[:, :128], across[:, 128:]], axis=0)
    constant = kinetic_scale * (shift_y * shift_y + shift_z * shift_z)
    return along + across + constant * field


def kinetic_x(field, high_ref, low_ref, shift):
    field_high, field_low = halves(field)
    dot = functools.partial(jnp.dot, preferred_element_type=f32)
    high = high_ref[...]
    moved = dot(high, field_high) + (dot(high, field_low) + dot(low_ref[...], field_high))
    return moved + (kinetic_scale * shift * shift) * field


def pack_body(
    index_ref, boxes_hbm, species_hbm, channels_hbm, proj_hbm, real_hbm, imag_hbm, out_ref, both_ref,
    boxes_ref, species_ref, channels_ref, proj_ref, rows_ref, done,
):
    place = index_ref[0] % 8
    core = index_ref[1] % 2
    copies = [
        pltpu.make_async_copy(boxes_hbm, boxes_ref, done.at[0]),
        pltpu.make_async_copy(species_hbm, species_ref, done.at[1]),
        pltpu.make_async_copy(channels_hbm, channels_ref, done.at[2]),
    ]
    copies += [pltpu.make_async_copy(proj_hbm.at[atom], proj_ref.at[atom], done.at[3 + atom]) for atom in range(4)]
    copies += [
        pltpu.make_async_copy(real_hbm, both_ref.at[pl.ds(0, 128)], done.at[7]),
        pltpu.make_async_copy(imag_hbm, both_ref.at[pl.ds(128, 128)], done.at[8]),
    ]
    for copy in copies:
        copy.start()
    sub = lax.broadcasted_iota(i32, (NPROJ, LANES), 0)
    lane = lax.broadcasted_iota(i32, (NPROJ, LANES), 1)
    cell = lane % BOX
    group = lane // BOX
    skew = (group + sub) % 8 * BOX + cell
    shift = (sub - group) % 8
    for copy in copies[:3]:
        copy.wait()
    facts = jnp.zeros((NPROJ, LANES), f32)
    for atom in range(4):
        for channel in range(NPROJ):
            here = (sub == channel) & (lane == atom)
            facts = jnp.where(here, channels_ref[atom, channel].astype(f32), facts)
        facts = jnp.where(lane == 4 + atom, species_ref[atom].astype(f32), facts)
        facts = jnp.where(lane == 8 + atom, boxes_ref[1, atom].astype(f32), facts)
        facts = jnp.where(lane == 12 + atom, boxes_ref[2, atom].astype(f32), facts)
        facts = jnp.where(lane == 16 + atom, (boxes_ref[0, atom] % 2).astype(f32), facts)
    for target in range(8):
        out_ref[target, 64:72, :] = facts
    for atom in range(4):
        copies[3 + atom].wait()
        last = shift * BOX + (cell + 256 - boxes_ref[2, atom]) % BOX
        for cut in range(BOX):
            start = pl.multiple_of((2 * cut + core) * LANES, LANES)
            tile = proj_ref[atom, :, pl.ds(start, LANES)]
            tile = jnp.take_along_axis(tile, skew, axis=1)
            tile = jnp.take_along_axis(tile, shift, axis=0)
            tile = jnp.take_along_axis(tile, last, axis=1)
            rows_ref[pl.ds(cut * 8, 8), :] = tile
            if cut == 0:
                rows_ref[pl.ds(128, 8), :] = tile
        odd = boxes_ref[0, atom] % 2
        for target in range(8):
            start = (2 * (target - place) - odd + 32) % BOX
            out_ref[target, pl.ds(atom * 16, 16), :] = rows_ref[pl.ds(pl.multiple_of(start * 8, 8), 16), :]
    for copy in copies[7:]:
        copy.wait()


def pick_body(index_ref, got_ref, boxes_ref):
    place = index_ref[0] % 8
    lane = lax.broadcasted_iota(i32, (NPROJ, LANES), 1)
    sub = lax.broadcasted_iota(i32, (NPROJ, LANES), 0)
    found = jnp.zeros((NPROJ, LANES), f32)
    for slot in range(8):
        facts = got_ref[slot, 64:72, :]
        here = lane // 4 == slot
        for row, offset in enumerate((8, 12, 16)):
            found = jnp.where(here & (sub == row), pltpu.roll(facts, (4 * slot - offset) % LANES, 1), found)
    odd = found[2:3, :].astype(i32)
    far = (2 * place + sub - 2) < 2 * (lane // 4) + odd
    boxes_ref[...] = jnp.where(sub < 2, found.astype(i32), jnp.where(far, 320, 0))


def merge_body(index_ref, here_ref, passed_ref, coupling_ref, proj_ref, table_ref, boxes_ref):
    place = index_ref[0] % 8
    lane = lax.broadcasted_iota(i32, (NPROJ, LANES), 1)
    sub = lax.broadcasted_iota(i32, (NPROJ, LANES), 0)
    zero = jnp.zeros((NPROJ, LANES), f32)
    gates, kind, first_y, first_z = zero, zero, zero, zero
    for slot in range(REACH):
        facts = zero

        @pl.when(slot <= place)
        def _():
            for half in range(2):
                proj_ref[half, pl.ds(slot * 64, 64), :] = here_ref[half, min(slot, 7), 0:64, :]
            boxes_ref[...] = here_ref[0, min(slot, 7), 64:72, :].astype(i32)

        @pl.when(slot > place)
        def _():
            for half in range(2):
                proj_ref[half, pl.ds(slot * 64, 64), :] = passed_ref[half, max(slot - 1, 0), 0:64, :]
            boxes_ref[...] = passed_ref[0, max(slot - 1, 0), 64:72, :].astype(i32)

        facts = boxes_ref[...].astype(f32)
        here = lane // 4 == slot

        def moved(offset):
            return jnp.where(here, pltpu.roll(facts, (4 * slot - offset) % LANES, 1), 0.0)

        gates += moved(0)
        kind += moved(4)
        first_y += moved(8)
        first_z += moved(12)
    for behind in range(2):
        source = (here_ref, passed_ref)[behind]
        odds = source[0, place, 64:72, :]
        for atom in range(4):
            odd = odds[0:1, 16 + atom : 17 + atom]
            keep = (odd < 0.5) if behind == 0 else (odd > 0.5)
            start = pl.multiple_of((place + behind) * 64 + atom * 16, 16)
            for half in range(2):
                rows = proj_ref[half, pl.ds(start, 8), :]
                proj_ref[half, pl.ds(start, 8), :] = jnp.where(keep, rows, 0.0)
                if behind == 1:
                    proj_ref[half, pl.ds(start + 8, 8), :] = zero
    gates += pltpu.roll(gates, IMAG, 1)
    kind += pltpu.roll(kind, IMAG, 1)
    for other in range(NPROJ):
        value = zero
        for which in range(KINDS):
            column = coupling_ref[which][:, other : other + 1]
            value = jnp.where(kind == float(which), column, value)
        table_ref[pl.ds(other * 8, 8), :] = value * gates * gates[other : other + 1, :]
    boxes_ref[...] = jnp.where(sub == 0, first_y, first_z).astype(i32)


def local_body(
    index_ref, vector_ref, both_ref, pot_ref, x_ref, y_ref, z_ref, out_ref, turn_ref, high_ref, low_ref
):
    slab = index_ref[0]
    field = both_ref[...]
    out = kinetic_yz(field, y_ref, z_ref, vector_ref[1], vector_ref[2])
    pot = pot_ref[...]
    out_ref[...] = out + jnp.concatenate([pot, pot], axis=0) * field
    row = lax.broadcasted_iota(i32, (128, LANES), 0)
    y = (row % NY).astype(f32)
    z = lax.broadcasted_iota(i32, (128, LANES), 1).astype(f32)
    for ahead in range(2):
        x = ((slab + 8 * ahead) % SLABS * 2 + row // NY).astype(f32)
        turns = vector_ref[0] * x / NX + vector_ref[1] * y / NY + vector_ref[2] * z / NZ
        turns = turns - jnp.floor(turns + 0.5)
        theta = (2.0 * math.pi) * turns
        turn_ref[2 * ahead] = jnp.cos(theta)
        turn_ref[2 * ahead + 1] = jnp.sin(theta)
    high, low = halves(x_ref[0] + vector_ref[0] * x_ref[1])
    high_ref[...] = high
    low_ref[...] = low


def turned_rows(real, imag, cosine, sine, field_ref, first_row):
    turned = (cosine * real - sine * imag, sine * real + cosine * imag)
    for part in range(2):
        for plane in range(2):
            base = first_row + (part * 2 + plane) * 80
            field_ref[pl.ds(base, 64), :] = turned[part][plane * 64 : plane * 64 + 64]
            field_ref[pl.ds(base + 64, 16), :] = turned[part][plane * 64 : plane * 64 + 16]


def project(boxes_ref, proj_ref, wide, far, atoms, field_ref, sums_ref):
    sums_ref[...] = jnp.zeros_like(sums_ref)
    cell = lax.broadcasted_iota(i32, (BOX, LANES), 1) % BOX

    def one(atom, carry):
        first_y = boxes_ref[0, atom]
        first_z = boxes_ref[1, atom]
        pick = (first_z + (cell + LANES - first_z) % BOX) % LANES
        total = [None, None]
        for plane in range(2):
            start = pl.multiple_of(atom // 4 * wide + atom % 4 * 16 + plane * 8, 8)
            beta = jnp.concatenate([proj_ref[0, pl.ds(start, 8), :], proj_ref[1, pl.ds(start, 8), :]], axis=0)
            base = first_y + boxes_ref[2 + plane, atom] if far else first_y
            for part in range(2):
                rows = field_ref[pl.ds((part * 2 + plane) * 80 + base, BOX), :]
                term = beta * jnp.take_along_axis(rows, pick, axis=1)
                total[part] = term if plane == 0 else total[part] + term
        for part in range(2):
            sums_ref[pl.ds(part * IMAG + atom, 1), :] = jnp.sum(total[part], axis=0, keepdims=True)
        return carry

    lax.fori_loop(0, atoms, one, 0, unroll=4)
    return lax.dot_general(
        group_matrix(), sums_ref[...], (((1,), (1,)), ((), ())), precision=highest, preferred_element_type=f32
    )


def row_sums(got_ref, row, kept):
    total = jnp.zeros((NPROJ, LANES), f32)
    for place in range(8):
        share = got_ref[row % 4 * 8 + place, 8:16, :]
        total += share if kept is None else jnp.where(kept(place), share, 0.0)
    return total


def first_coefs(slab, got_ref):
    group = lax.broadcasted_iota(i32, (NPROJ, LANES), 1) % IMAG // 4
    own = row_sums(got_ref, slab // 8, None)
    before = row_sums(got_ref, slab // 8 + 3, None)
    return jnp.where(group <= slab % 8, own, pltpu.roll(before, 4, 1))


def second_coefs(slab, got_ref):
    group = lax.broadcasted_iota(i32, (NPROJ, LANES), 1) % IMAG // 4
    row = slab // 8

    def own(place):
        return group <= place

    def passed(place):
        return (group > place) & (group < REACH)

    here = row_sums(got_ref, row, own) + pltpu.roll(row_sums(got_ref, row + 1, passed), LANES - 4, 1)
    before = pltpu.roll(row_sums(got_ref, row + 3, own), 4, 1) + row_sums(got_ref, row, passed)
    return jnp.where(group <= slab % 8, here, jnp.where(group < REACH, before, 0.0))


def spread(coef, boxes_ref, proj_ref, table_ref, turn_ref, place_ref, dual_ref):
    dual = jnp.zeros((NPROJ, LANES), f32)
    for other in range(NPROJ):
        dual += table_ref[pl.ds(other * 8, 8), :] * coef[other : other + 1, :]
    dual_ref[...] = lax.dot_general(
        dual, group_matrix(), (((0,), (0,)), ((), ())), precision=highest, preferred_element_type=f32
    )
    place_ref[...] = jnp.zeros_like(place_ref)
    left = lax.broadcasted_iota(i32, (256, 256), 0)
    right = lax.broadcasted_iota(i32, (256, 256), 1)
    gather = ((left // LANES == right // LANES) & (left % BOX == right % BOX)).astype(f32).astype(jnp.bfloat16)
    wide = lax.broadcasted_iota(i32, (8, 2 * LANES), 1) % LANES
    dot = functools.partial(jnp.dot, preferred_element_type=f32)
    for distance in range(REACH):
        rows = []
        for half in range(2):
            for atom in range(4 * distance, 4 * distance + 4):
                beta = proj_ref[half, pl.ds(atom * 16, 16), :]
                real = beta * dual_ref[pl.ds(atom, 1), :]
                imag = beta * dual_ref[pl.ds(IMAG + atom, 1), :]
                rows.append(jnp.concatenate([real, imag], axis=1))
        high, low = halves(jnp.concatenate(rows, axis=0))
        value = dot(high, gather) + dot(low, gather)
        for atom in range(4 * distance, 4 * distance + 4):
            first_y = boxes_ref[0, atom]
            first_z = boxes_ref[1, atom]
            inside = (wide + LANES - first_z) % LANES < BOX
            for plane in range(2):
                parts = []
                for half in range(2):
                    start = half * 64 + (atom % 4) * 16 + plane * 8
                    parts.append(jnp.where(inside, value[start : start + 8], 0.0))
                both = jnp.concatenate(parts, axis=0)
                place_ref[pl.ds(plane * 80 + first_y, BOX), :] += both[:, :LANES]
                place_ref[pl.ds(160 + plane * 80 + first_y, BOX), :] += both[:, LANES:]
    for block in range(4):
        place_ref[pl.ds(block * 80, 16), :] += place_ref[pl.ds(block * 80 + 64, 16), :]
    back_real = jnp.concatenate([place_ref[pl.ds(0, 64), :], place_ref[pl.ds(80, 64), :]], axis=0)
    back_imag = jnp.concatenate([place_ref[pl.ds(160, 64), :], place_ref[pl.ds(240, 64), :]], axis=0)
    cosine, sine = turn_ref[0], turn_ref[1]
    return cosine * back_real + sine * back_imag, cosine * back_imag - sine * back_real


def columns(field_ref, out_ref):
    for y in range(2):
        for part in range(2):
            for plane in range(2):
                row = y * 4 + part * 2 + plane
                start = part * 128 + plane * 64 + y
                out_ref[:, row, :] = field_ref[pl.ds(start, SLABS, stride=2), :]


def unpack(got_ref, first_row, field_ref):
    for y in range(2):
        for part in range(2):
            for plane in range(2):
                row = y * 4 + part * 2 + plane
                start = part * 128 + plane * 64 + y
                field_ref[pl.ds(start, SLABS, stride=2), :] = got_ref[:, first_row + row, :]


def coef_body(boxes_ref, proj_ref, both_ref, next_ref, turn_ref, out_ref, field_ref, sums_ref):
    columns(both_ref, out_ref)
    for ahead, ref in enumerate((both_ref, next_ref)):
        turned_rows(
            ref[0:128, :], ref[128:256, :], turn_ref[2 * ahead], turn_ref[2 * ahead + 1], field_ref, 320 * ahead
        )
    coef = project(boxes_ref, proj_ref, 72, True, 32, field_ref, sums_ref)
    out_ref[:, 8:16, :] = jnp.broadcast_to(coef[None], (SLABS, 8, LANES))


def rest_body(
    index_ref, vector_ref, boxes_ref, proj_ref, table_ref, got_ref, turn_ref, local_ref, high_ref, low_ref,
    rest_ref, moved_ref, out_ref, place_ref, dual_ref,
):
    field = got_ref[:, 0:8, :].reshape(256, LANES)
    moved = kinetic_x(field, high_ref, low_ref, vector_ref[0])
    moved_ref[...] = moved
    out_ref[:, 8:16, :] = moved.reshape(SLABS, 8, LANES)
    coef = first_coefs(index_ref[0], got_ref)
    far_real, far_imag = spread(coef, boxes_ref, proj_ref, table_ref, turn_ref, place_ref, dual_ref)
    rest_ref[0:128, :] = local_ref[0:128, :] + far_real
    rest_ref[128:256, :] = local_ref[128:256, :] + far_imag
    columns(rest_ref, out_ref)


def first_body(
    vector_ref, boxes_ref, proj_ref, got_ref, turn_ref, rest_ref, moved_ref, high_ref, low_ref,
    first_ref, out_ref, field_ref, sums_ref,
):
    field = got_ref[:, 0:8, :].reshape(256, LANES) + moved_ref[...]
    out_ref[:, 0:8, :] = kinetic_x(field, high_ref, low_ref, vector_ref[0]).reshape(SLABS, 8, LANES)
    unpack(got_ref, 8, first_ref)
    real = first_ref[0:128, :] + rest_ref[0:128, :]
    imag = first_ref[128:256, :] + rest_ref[128:256, :]
    first_ref[0:128, :] = real
    first_ref[128:256, :] = imag
    turned_rows(real, imag, turn_ref[0], turn_ref[1], field_ref, 0)
    coef = project(boxes_ref, proj_ref, 64, False, 4 * REACH, field_ref, sums_ref)
    out_ref[:, 8:16, :] = jnp.broadcast_to(coef[None], (SLABS, 8, LANES))


def second_body(vector_ref, first_ref, pot_ref, y_ref, z_ref, out_ref):
    field = first_ref[...]
    pot = pot_ref[...]
    near = kinetic_yz(field, y_ref, z_ref, vector_ref[1], vector_ref[2])
    out_ref[...] = near + jnp.concatenate([pot, pot], axis=0) * field


def final_body(
    index_ref, occupation_ref, boxes_ref, proj_ref, table_ref, got_ref, turn_ref, both_ref, first_ref, near_ref,
    new_real_ref, new_imag_ref, out_ref, field_ref, place_ref, dual_ref,
):
    unpack(got_ref, 0, field_ref)
    coef = second_coefs(index_ref[0], got_ref)
    far_real, far_imag = spread(coef, boxes_ref, proj_ref, table_ref, turn_ref, place_ref, dual_ref)
    half = 0.5 * time_step * time_step
    second_real = near_ref[0:128, :] + field_ref[0:128, :] + far_real
    second_imag = near_ref[128:256, :] + field_ref[128:256, :] + far_imag
    new_real = both_ref[0:128, :] + time_step * first_ref[128:256, :] - half * second_real
    new_imag = both_ref[128:256, :] - time_step * first_ref[0:128, :] - half * second_imag
    new_real_ref[...] = new_real
    new_imag_ref[...] = new_imag
    weighted = occupation_ref[0] * (new_real * new_real + new_imag * new_imag)
    weighted = weighted.reshape(2, BANDS, 4, LANES)
    for plane in range(2):
        out_ref[:, pl.ds(plane * 4, 4), :] = weighted[plane]


def smem():
    return pl.BlockSpec(memory_space=pltpu.SMEM)


def vmem():
    return pl.BlockSpec(memory_space=pltpu.VMEM)


def call(body, scalars, arrays, outs, scratch=()):
    several = isinstance(outs, tuple)
    return pl.pallas_call(
        body,
        out_shape=outs,
        in_specs=[smem()] * len(scalars) + [vmem()] * len(arrays),
        out_specs=tuple(vmem() for _ in outs) if several else vmem(),
        scratch_shapes=list(scratch),
        compiler_params=pltpu.CompilerParams(vmem_limit_bytes=24 * 1024 * 1024),
    )(*scalars, *arrays)


def shape(*dims, dtype=f32):
    return jax.ShapeDtypeStruct(dims, dtype)


def exchange(value, axis):
    return lax.all_to_all(value, axis, split_axis=0, concat_axis=0, tiled=True)


def per_device(
    psi_real, psi_imag, potential, vector_potential, occupation, projectors, box_offsets, species, channels, coupling
):
    x_table, y_table, z_table = (jnp.asarray(table) for table in tables())
    index = jnp.stack([lax.axis_index("fft"), lax.axis_index("band")]).astype(i32)
    real = psi_real.reshape(128, LANES)
    imag = psi_imag.reshape(128, LANES)
    pot = potential.reshape(128, LANES)
    matrix = jax.ShapeDtypeStruct((256, 256), jnp.bfloat16)
    window = pltpu.VMEM((320, LANES), f32)
    square = pltpu.VMEM((128, LANES), f32)
    whole = pltpu.VMEM((256, LANES), f32)

    anywhere = pl.BlockSpec(memory_space=pltpu.HBM)
    slices, both = pl.pallas_call(
        pack_body,
        out_shape=(shape(8, 72, LANES), shape(256, LANES)),
        in_specs=[smem()] + [anywhere] * 6,
        out_specs=(vmem(), vmem()),
        scratch_shapes=[
            pltpu.SMEM((3, 4), i32), pltpu.SMEM((4,), i32), pltpu.SMEM((4, 8), i32),
            pltpu.VMEM((4, 8, 4096), f32), pltpu.VMEM((136, LANES), f32), pltpu.SemaphoreType.DMA((9,)),
        ],
        compiler_params=pltpu.CompilerParams(vmem_limit_bytes=60 * 1024 * 1024),
    )(index, box_offsets, species, channels, projectors, real, imag)
    ahead = lax.ppermute(both, "fft", [(i, (i + 24) % SLABS) for i in range(SLABS)])
    rows = [list(range(8 * x, 8 * x + 8)) for x in range(4)]
    got = lax.all_to_all(slices, "fft", split_axis=0, concat_axis=0, tiled=True, axis_index_groups=rows)
    local, turn, high, low = call(
        local_body, (index, vector_potential), (both, pot, x_table, y_table, z_table),
        (shape(256, LANES), shape(4, 128, LANES), matrix, matrix),
    )
    got, ahead, local, turn, high, low = lax.optimization_barrier((got, ahead, local, turn, high, low))
    chips = [[2 * y, 2 * y + 1] for y in range(8)]
    gathered = lax.all_gather(got, "band", axis_index_groups=chips)
    corners = call(pick_body, (index,), (got,), shape(8, LANES, dtype=i32))
    passed = lax.ppermute(got, "fft", [(i, (i + 8) % SLABS) for i in range(SLABS)])
    shares = call(
        coef_body, (corners,), (gathered.reshape(2, 576, LANES), both, ahead, turn), shape(SLABS, 16, LANES),
        (pltpu.VMEM((640, LANES), f32), square),
    )
    shares, passed = lax.optimization_barrier((shares, passed))
    passed = lax.all_gather(passed, "band", axis_index_groups=chips)
    got = exchange(shares, "fft")
    beta, table, boxes = call(
        merge_body, (index,), (gathered, passed, coupling),
        (shape(2, 576, LANES), shape(64, LANES), shape(8, LANES, dtype=i32)),
    )
    rest, moved, shares = call(
        rest_body, (index, vector_potential, boxes), (beta, table, got, turn, local, high, low),
        (shape(256, LANES), shape(256, LANES), shape(SLABS, 16, LANES)), (window, square),
    )
    got = exchange(shares, "fft")
    first, shares = call(
        first_body, (vector_potential, boxes), (beta, got, turn, rest, moved, high, low),
        (shape(256, LANES), shape(SLABS, 16, LANES)), (window, square),
    )
    got = exchange(shares, "fft")
    near = call(second_body, (vector_potential,), (first, pot, y_table, z_table), shape(256, LANES))
    new_real, new_imag, weighted = call(
        final_body, (index, occupation, boxes), (beta, table, got, turn, both, first, near),
        (shape(128, LANES), shape(128, LANES), shape(BANDS, 8, LANES)), (whole, window, square),
    )
    density = jnp.sum(exchange(weighted, "band"), axis=0).reshape(2, 4, LANES)
    grid = (1, 2, NY, NZ)
    return new_real.reshape(grid), new_imag.reshape(grid), density


def solution(mesh):
    placed = (
        P("band", "fft", None, None),
        P("band", "fft", None, None),
        P("fft", None, None),
        P(),
        P("band"),
        P("fft", None, None),
        P(None, "fft"),
        P("fft"),
        P("fft", None),
        P(),
    )
    return jax.shard_map(
        per_device,
        mesh=mesh,
        in_specs=placed,
        out_specs=(
            P("band", "fft", None, None),
            P("band", "fft", None, None),
            P("fft", "band", None),
        ),
        check_vma=False,
    )
```

```python
import functools
import math

import jax
import jax.numpy as jnp
import numpy as np
from jax import lax
from jax.experimental import pallas as pl
from jax.experimental.pallas import tpu as pltpu
from jax.sharding import PartitionSpec as P

NX = 64
NY = 64
NZ = 128
BOX = 16
NPROJ = 8
SLABS = 32
BANDS = 16
REACH = 9
KINDS = 4
LANES = 128
IMAG = 64

time_step = 0.01
kinetic_scale = 0.5 * (2.0 * math.pi / 38.0) ** 2
highest = lax.Precision.HIGHEST
f32 = jnp.float32
i32 = jnp.int32


def circulant(length):
    modes = np.arange(length)
    modes = np.where(modes < length // 2, modes, modes - length).astype(np.float64)
    steps = np.arange(length)
    wave = np.exp(2j * np.pi * np.outer(steps, modes) / length) / length
    apart = (steps[:, None] - steps[None, :]) % length
    return (wave @ modes**2)[apart] * kinetic_scale, (wave @ modes)[apart] * 2.0 * kinetic_scale


def blocks(matrix):
    return np.array([[matrix.real, -matrix.imag], [matrix.imag, matrix.real]])


def along_x(matrix):
    whole = blocks(matrix).reshape(2, 2, SLABS, 2, SLABS, 2)
    out = np.einsum("cdipjq,yz->iycpjzdq", whole, np.eye(2))
    return out.reshape(256, 256).astype(np.float32)


def along_y(matrix):
    out = np.einsum("cdyz,pq->cpydqz", blocks(matrix), np.eye(2))
    return out.reshape(256, 256).astype(np.float32)


def along_z(matrix):
    return np.einsum("cdyz->dzcy", blocks(matrix)).reshape(256, 256).astype(np.float32)


def tables():
    x2, x1 = circulant(NX)
    y2, y1 = circulant(NY)
    z2, z1 = circulant(NZ)
    return (
        np.stack([along_x(x2), along_x(x1)]),
        np.stack([along_y(y2), along_y(y1)]),
        np.stack([along_z(z2), along_z(z1)]),
    )


def halves(value):
    high = value.astype(jnp.bfloat16)
    low = (value - high.astype(f32)).astype(jnp.bfloat16)
    return high, low


def dot3(left, right):
    left_high, left_low = halves(left)
    right_high, right_low = halves(right)
    dot = functools.partial(jnp.dot, preferred_element_type=f32)
    return dot(left_high, right_high) + (dot(left_high, right_low) + dot(left_low, right_high))


def group_matrix():
    row = lax.broadcasted_iota(i32, (NPROJ, LANES), 0)
    lane = lax.broadcasted_iota(i32, (NPROJ, LANES), 1)
    return (lane // BOX == row).astype(f32)


def kinetic_yz(field, y_ref, z_ref, shift_y, shift_z):
    along = dot3(y_ref[0] + shift_y * y_ref[1], field)
    wide = jnp.concatenate([field[:128], field[128:]], axis=1)
    across = dot3(wide, z_ref[0] + shift_z * z_ref[1])
    across = jnp.concatenate([across[:, :128], across[:, 128:]], axis=0)
    constant = kinetic_scale * (shift_y * shift_y + shift_z * shift_z)
    return along + across + constant * field


def kinetic_x(field, high_ref, low_ref, shift):
    field_high, field_low = halves(field)
    dot = functools.partial(jnp.dot, preferred_element_type=f32)
    high = high_ref[...]
    moved = dot(high, field_high) + (dot(high, field_low) + dot(low_ref[...], field_high))
    return moved + (kinetic_scale * shift * shift) * field


def pack_body(
    boxes_hbm, species_hbm, channels_hbm, proj_hbm, real_hbm, imag_hbm, out_ref, both_ref,
    boxes_ref, species_ref, channels_ref, proj_ref, rows_ref, done,
):
    place = lax.axis_index("fft") % 8
    core = lax.axis_index("band") % 2
    copies = [
        pltpu.make_async_copy(boxes_hbm, boxes_ref, done.at[0]),
        pltpu.make_async_copy(species_hbm, species_ref, done.at[1]),
        pltpu.make_async_copy(channels_hbm, channels_ref, done.at[2]),
    ]
    copies += [pltpu.make_async_copy(proj_hbm.at[atom], proj_ref.at[atom], done.at[3 + atom]) for atom in range(4)]
    copies += [
        pltpu.make_async_copy(real_hbm, both_ref.at[pl.ds(0, 128)], done.at[7]),
        pltpu.make_async_copy(imag_hbm, both_ref.at[pl.ds(128, 128)], done.at[8]),
    ]
    for copy in copies:
        copy.start()
    sub = lax.broadcasted_iota(i32, (NPROJ, LANES), 0)
    lane = lax.broadcasted_iota(i32, (NPROJ, LANES), 1)
    cell = lane % BOX
    group = lane // BOX
    skew = ((group + sub) & 7) * BOX + cell
    shift = (sub - group) & 7
    for copy in copies[:3]:
        copy.wait()
    facts = jnp.zeros((NPROJ, LANES), f32)
    for atom in range(4):
        for channel in range(NPROJ):
            here = (sub == channel) & (lane == atom)
            facts = jnp.where(here, channels_ref[atom, channel].astype(f32), facts)
        facts = jnp.where(lane == 4 + atom, species_ref[atom].astype(f32), facts)
        facts = jnp.where(lane == 8 + atom, boxes_ref[1, atom].astype(f32), facts)
        facts = jnp.where(lane == 12 + atom, boxes_ref[2, atom].astype(f32), facts)
        facts = jnp.where(lane == 16 + atom, ((boxes_ref[0, atom] & 1)).astype(f32), facts)
    for target in range(8):
        out_ref[target, 64:72, :] = facts
    for atom in range(4):
        copies[3 + atom].wait()
        last = shift * BOX + ((cell - boxes_ref[2, atom]) & (BOX - 1))
        for cut in range(BOX):
            start = pl.multiple_of((2 * cut + core) * LANES, LANES)
            tile = proj_ref[atom, :, pl.ds(start, LANES)]
            tile = jnp.take_along_axis(tile, skew, axis=1)
            tile = jnp.take_along_axis(tile, shift, axis=0)
            tile = jnp.take_along_axis(tile, last, axis=1)
            rows_ref[pl.ds(cut * 8, 8), :] = tile
            if cut == 0:
                rows_ref[pl.ds(128, 8), :] = tile
        odd = (boxes_ref[0, atom] & 1)
        for target in range(8):
            start = (2 * (target - place) - odd) & (BOX - 1)
            out_ref[target, pl.ds(atom * 16, 16), :] = rows_ref[pl.ds(pl.multiple_of(start * 8, 8), 16), :]
    for copy in copies[7:]:
        copy.wait()


def pick_body(got_ref, boxes_ref):
    place = lax.axis_index("fft") % 8
    lane = lax.broadcasted_iota(i32, (NPROJ, LANES), 1)
    sub = lax.broadcasted_iota(i32, (NPROJ, LANES), 0)
    found = jnp.zeros((NPROJ, LANES), f32)
    for slot in range(8):
        facts = got_ref[slot, 64:72, :]
        here = lane // 4 == slot
        for row, offset in enumerate((8, 12, 16)):
            found = jnp.where(here & (sub == row), pltpu.roll(facts, (4 * slot - offset) % LANES, 1), found)
    odd = found[2:3, :].astype(i32)
    far = (2 * place + sub - 2) < 2 * (lane // 4) + odd
    boxes_ref[...] = jnp.where(sub < 2, found.astype(i32), jnp.where(far, 320, 0))


def merge_body(here_ref, passed_ref, coupling_ref, proj_ref, table_ref, boxes_ref):
    place = lax.axis_index("fft") % 8
    lane = lax.broadcasted_iota(i32, (NPROJ, LANES), 1)
    sub = lax.broadcasted_iota(i32, (NPROJ, LANES), 0)
    zero = jnp.zeros((NPROJ, LANES), f32)
    gates, kind, first_y, first_z = zero, zero, zero, zero
    for slot in range(REACH):
        facts = zero

        @pl.when(slot <= place)
        def _():
            for half in range(2):
                proj_ref[half, pl.ds(slot * 64, 64), :] = here_ref[half, min(slot, 7), 0:64, :]
            boxes_ref[...] = here_ref[0, min(slot, 7), 64:72, :].astype(i32)

        @pl.when(slot > place)
        def _():
            for half in range(2):
                proj_ref[half, pl.ds(slot * 64, 64), :] = passed_ref[half, max(slot - 1, 0), 0:64, :]
            boxes_ref[...] = passed_ref[0, max(slot - 1, 0), 64:72, :].astype(i32)

        facts = boxes_ref[...].astype(f32)
        here = lane // 4 == slot

        def moved(offset):
            return jnp.where(here, pltpu.roll(facts, (4 * slot - offset) % LANES, 1), 0.0)

        gates += moved(0)
        kind += moved(4)
        first_y += moved(8)
        first_z += moved(12)
    for behind in range(2):
        source = (here_ref, passed_ref)[behind]
        odds = source[0, place, 64:72, :]
        for atom in range(4):
            odd = odds[0:1, 16 + atom : 17 + atom]
            keep = (odd < 0.5) if behind == 0 else (odd > 0.5)
            start = pl.multiple_of((place + behind) * 64 + atom * 16, 16)
            for half in range(2):
                rows = proj_ref[half, pl.ds(start, 8), :]
                proj_ref[half, pl.ds(start, 8), :] = jnp.where(keep, rows, 0.0)
                if behind == 1:
                    proj_ref[half, pl.ds(start + 8, 8), :] = zero
    gates += pltpu.roll(gates, IMAG, 1)
    kind += pltpu.roll(kind, IMAG, 1)
    for other in range(NPROJ):
        value = zero
        for which in range(KINDS):
            column = coupling_ref[which][:, other : other + 1]
            value = jnp.where(kind == float(which), column, value)
        table_ref[pl.ds(other * 8, 8), :] = value * gates * gates[other : other + 1, :]
    boxes_ref[...] = jnp.where(sub == 0, first_y, first_z).astype(i32)


def phase_body(vector_ref, turn_ref):
    slab = lax.axis_index("fft")
    row = lax.broadcasted_iota(i32, (128, LANES), 0)
    y = (row % NY).astype(f32)
    z = lax.broadcasted_iota(i32, (128, LANES), 1).astype(f32)
    for ahead in range(2):
        x = ((slab + 8 * ahead) % SLABS * 2 + row // NY).astype(f32)
        turns = vector_ref[0] * x / NX + vector_ref[1] * y / NY + vector_ref[2] * z / NZ
        turns = turns - jnp.floor(turns + 0.5)
        theta = (2.0 * math.pi) * turns
        turn_ref[2 * ahead] = jnp.cos(theta)
        turn_ref[2 * ahead + 1] = jnp.sin(theta)


def local_body(
    vector_ref, both_ref, pot_ref, x_ref, y_ref, z_ref, out_ref, high_ref, low_ref
):
    field = both_ref[...]
    out = kinetic_yz(field, y_ref, z_ref, vector_ref[1], vector_ref[2])
    pot = pot_ref[...]
    out_ref[...] = out + jnp.concatenate([pot, pot], axis=0) * field
    high, low = halves(x_ref[0] + vector_ref[0] * x_ref[1])
    high_ref[...] = high
    low_ref[...] = low


def turned_rows(real, imag, cosine, sine, field_ref, first_row):
    turned = (cosine * real - sine * imag, sine * real + cosine * imag)
    for part in range(2):
        for plane in range(2):
            base = first_row + (part * 2 + plane) * 80
            field_ref[pl.ds(base, 64), :] = turned[part][plane * 64 : plane * 64 + 64]
            field_ref[pl.ds(base + 64, 16), :] = turned[part][plane * 64 : plane * 64 + 16]


def project(boxes_ref, proj_ref, wide, far, atoms, field_ref, sums_ref):
    sums_ref[...] = jnp.zeros_like(sums_ref)
    cell = lax.broadcasted_iota(i32, (BOX, LANES), 1) % BOX

    def one(atom, carry):
        first_y = boxes_ref[0, atom]
        first_z = boxes_ref[1, atom]
        pick = (first_z + ((cell - first_z) & (BOX - 1))) & (LANES - 1)
        total = [None, None]
        for plane in range(2):
            start = pl.multiple_of(atom // 4 * wide + atom % 4 * 16 + plane * 8, 8)
            beta = jnp.concatenate([proj_ref[0, pl.ds(start, 8), :], proj_ref[1, pl.ds(start, 8), :]], axis=0)
            base = first_y + boxes_ref[2 + plane, atom] if far else first_y
            for part in range(2):
                rows = field_ref[pl.ds((part * 2 + plane) * 80 + base, BOX), :]
                term = beta * jnp.take_along_axis(rows, pick, axis=1)
                total[part] = term if plane == 0 else total[part] + term
        for part in range(2):
            sums_ref[pl.ds(part * IMAG + atom, 1), :] = jnp.sum(total[part], axis=0, keepdims=True)
        return carry

    lax.fori_loop(0, atoms, one, 0, unroll=True)
    return lax.dot_general(
        group_matrix(), sums_ref[...], (((1,), (1,)), ((), ())), precision=highest, preferred_element_type=f32
    )


def row_sums(got_ref, row, kept):
    total = jnp.zeros((NPROJ, LANES), f32)
    for place in range(8):
        share = got_ref[row % 4 * 8 + place, 8:16, :]
        total += share if kept is None else jnp.where(kept(place), share, 0.0)
    return total


def first_coefs(slab, got_ref):
    group = lax.broadcasted_iota(i32, (NPROJ, LANES), 1) % IMAG // 4
    own = row_sums(got_ref, slab // 8, None)
    before = row_sums(got_ref, slab // 8 + 3, None)
    return jnp.where(group <= slab % 8, own, pltpu.roll(before, 4, 1))


def second_coefs(slab, got_ref):
    group = lax.broadcasted_iota(i32, (NPROJ, LANES), 1) % IMAG // 4
    row = slab // 8

    def own(place):
        return group <= place

    def passed(place):
        return (group > place) & (group < REACH)

    here = row_sums(got_ref, row, own) + pltpu.roll(row_sums(got_ref, row + 1, passed), LANES - 4, 1)
    before = pltpu.roll(row_sums(got_ref, row + 3, own), 4, 1) + row_sums(got_ref, row, passed)
    return jnp.where(group <= slab % 8, here, jnp.where(group < REACH, before, 0.0))


def spread(coef, boxes_ref, proj_ref, table_ref, turn_ref, place_ref, dual_ref):
    dual = jnp.zeros((NPROJ, LANES), f32)
    for other in range(NPROJ):
        dual += table_ref[pl.ds(other * 8, 8), :] * coef[other : other + 1, :]
    dual_ref[...] = lax.dot_general(
        dual, group_matrix(), (((0,), (0,)), ((), ())), precision=highest, preferred_element_type=f32
    )
    place_ref[...] = jnp.zeros_like(place_ref)
    left = lax.broadcasted_iota(i32, (256, 256), 0)
    right = lax.broadcasted_iota(i32, (256, 256), 1)
    gather = ((left // LANES == right // LANES) & (left % BOX == right % BOX)).astype(f32).astype(jnp.bfloat16)
    wide = lax.broadcasted_iota(i32, (8, 2 * LANES), 1) % LANES
    dot = functools.partial(jnp.dot, preferred_element_type=f32)
    for distance in range(REACH):
        rows = []
        for half in range(2):
            for atom in range(4 * distance, 4 * distance + 4):
                beta = proj_ref[half, pl.ds(atom * 16, 16), :]
                real = beta * dual_ref[pl.ds(atom, 1), :]
                imag = beta * dual_ref[pl.ds(IMAG + atom, 1), :]
                rows.append(jnp.concatenate([real, imag], axis=1))
        high, low = halves(jnp.concatenate(rows, axis=0))
        value = dot(high, gather) + dot(low, gather)
        for atom in range(4 * distance, 4 * distance + 4):
            first_y = boxes_ref[0, atom]
            first_z = boxes_ref[1, atom]
            inside = ((wide - first_z) & (LANES - 1)) < BOX
            for plane in range(2):
                parts = []
                for half in range(2):
                    start = half * 64 + (atom % 4) * 16 + plane * 8
                    parts.append(jnp.where(inside, value[start : start + 8], 0.0))
                both = jnp.concatenate(parts, axis=0)
                place_ref[pl.ds(plane * 80 + first_y, BOX), :] += both[:, :LANES]
                place_ref[pl.ds(160 + plane * 80 + first_y, BOX), :] += both[:, LANES:]
    for block in range(4):
        place_ref[pl.ds(block * 80, 16), :] += place_ref[pl.ds(block * 80 + 64, 16), :]
    back_real = jnp.concatenate([place_ref[pl.ds(0, 64), :], place_ref[pl.ds(80, 64), :]], axis=0)
    back_imag = jnp.concatenate([place_ref[pl.ds(160, 64), :], place_ref[pl.ds(240, 64), :]], axis=0)
    cosine, sine = turn_ref[0], turn_ref[1]
    return cosine * back_real + sine * back_imag, cosine * back_imag - sine * back_real


def columns(field_ref, out_ref):
    for y in range(2):
        for part in range(2):
            for plane in range(2):
                row = y * 4 + part * 2 + plane
                start = part * 128 + plane * 64 + y
                out_ref[:, row, :] = field_ref[pl.ds(start, SLABS, stride=2), :]


def unpack(got_ref, first_row, field_ref):
    for y in range(2):
        for part in range(2):
            for plane in range(2):
                row = y * 4 + part * 2 + plane
                start = part * 128 + plane * 64 + y
                field_ref[pl.ds(start, SLABS, stride=2), :] = got_ref[:, first_row + row, :]


def coef_body(boxes_ref, proj_ref, both_ref, next_ref, turn_ref, out_ref, field_ref, sums_ref):
    columns(both_ref, out_ref)
    for ahead, ref in enumerate((both_ref, next_ref)):
        turned_rows(
            ref[0:128, :], ref[128:256, :], turn_ref[2 * ahead], turn_ref[2 * ahead + 1], field_ref, 320 * ahead
        )
    coef = project(boxes_ref, proj_ref, 72, True, 32, field_ref, sums_ref)
    out_ref[:, 8:16, :] = jnp.broadcast_to(coef[None], (SLABS, 8, LANES))


def rest_body(
    vector_ref, boxes_ref, proj_ref, table_ref, got_ref, turn_ref, local_ref, high_ref, low_ref,
    rest_ref, moved_ref, out_ref, place_ref, dual_ref,
):
    field = got_ref[:, 0:8, :].reshape(256, LANES)
    moved = kinetic_x(field, high_ref, low_ref, vector_ref[0])
    moved_ref[...] = moved
    out_ref[:, 8:16, :] = moved.reshape(SLABS, 8, LANES)
    coef = first_coefs(lax.axis_index("fft"), got_ref)
    far_real, far_imag = spread(coef, boxes_ref, proj_ref, table_ref, turn_ref, place_ref, dual_ref)
    rest_ref[0:128, :] = local_ref[0:128, :] + far_real
    rest_ref[128:256, :] = local_ref[128:256, :] + far_imag
    columns(rest_ref, out_ref)


def first_body(
    vector_ref, boxes_ref, proj_ref, got_ref, turn_ref, rest_ref, moved_ref, high_ref, low_ref,
    first_ref, out_ref, field_ref, sums_ref,
):
    field = got_ref[:, 0:8, :].reshape(256, LANES) + moved_ref[...]
    out_ref[:, 0:8, :] = kinetic_x(field, high_ref, low_ref, vector_ref[0]).reshape(SLABS, 8, LANES)
    unpack(got_ref, 8, first_ref)
    real = first_ref[0:128, :] + rest_ref[0:128, :]
    imag = first_ref[128:256, :] + rest_ref[128:256, :]
    first_ref[0:128, :] = real
    first_ref[128:256, :] = imag
    turned_rows(real, imag, turn_ref[0], turn_ref[1], field_ref, 0)
    coef = project(boxes_ref, proj_ref, 64, False, 4 * REACH, field_ref, sums_ref)
    out_ref[:, 8:16, :] = jnp.broadcast_to(coef[None], (SLABS, 8, LANES))


def second_body(vector_ref, first_ref, pot_ref, y_ref, z_ref, out_ref):
    field = first_ref[...]
    pot = pot_ref[...]
    near = kinetic_yz(field, y_ref, z_ref, vector_ref[1], vector_ref[2])
    out_ref[...] = near + jnp.concatenate([pot, pot], axis=0) * field


def final_body(
    occupation_ref, boxes_ref, proj_ref, table_ref, got_ref, turn_ref, both_ref, first_ref, near_ref,
    new_real_ref, new_imag_ref, out_ref, field_ref, place_ref, dual_ref,
):
    unpack(got_ref, 0, field_ref)
    coef = second_coefs(lax.axis_index("fft"), got_ref)
    far_real, far_imag = spread(coef, boxes_ref, proj_ref, table_ref, turn_ref, place_ref, dual_ref)
    half = 0.5 * time_step * time_step
    second_real = near_ref[0:128, :] + field_ref[0:128, :] + far_real
    second_imag = near_ref[128:256, :] + field_ref[128:256, :] + far_imag
    new_real = both_ref[0:128, :] + time_step * first_ref[128:256, :] - half * second_real
    new_imag = both_ref[128:256, :] - time_step * first_ref[0:128, :] - half * second_imag
    new_real_ref[...] = new_real
    new_imag_ref[...] = new_imag
    weighted = occupation_ref[0] * (new_real * new_real + new_imag * new_imag)
    weighted = weighted.reshape(2, BANDS, 4, LANES)
    for plane in range(2):
        out_ref[:, pl.ds(plane * 4, 4), :] = weighted[plane]


def smem():
    return pl.BlockSpec(memory_space=pltpu.SMEM)


def vmem():
    return pl.BlockSpec(memory_space=pltpu.VMEM)


def call(body, scalars, arrays, outs, scratch=()):
    several = isinstance(outs, tuple)
    return pl.pallas_call(
        body,
        out_shape=outs,
        in_specs=[smem()] * len(scalars) + [vmem()] * len(arrays),
        out_specs=tuple(vmem() for _ in outs) if several else vmem(),
        scratch_shapes=list(scratch),
        compiler_params=pltpu.CompilerParams(vmem_limit_bytes=24 * 1024 * 1024),
    )(*scalars, *arrays)


def shape(*dims, dtype=f32):
    return jax.ShapeDtypeStruct(dims, dtype)


def exchange(value, axis):
    return lax.all_to_all(value, axis, split_axis=0, concat_axis=0, tiled=True)


def per_device(
    psi_real, psi_imag, potential, vector_potential, occupation, projectors, box_offsets, species, channels, coupling
):
    x_table, y_table, z_table = (jnp.asarray(table) for table in tables())
    real = psi_real.reshape(128, LANES)
    imag = psi_imag.reshape(128, LANES)
    pot = potential.reshape(128, LANES)
    matrix = jax.ShapeDtypeStruct((256, 256), jnp.bfloat16)
    window = pltpu.VMEM((320, LANES), f32)
    square = pltpu.VMEM((128, LANES), f32)
    whole = pltpu.VMEM((256, LANES), f32)

    anywhere = pl.BlockSpec(memory_space=pltpu.HBM)
    slices, both = pl.pallas_call(
        pack_body,
        out_shape=(shape(8, 72, LANES), shape(256, LANES)),
        in_specs=[anywhere] * 6,
        out_specs=(vmem(), vmem()),
        scratch_shapes=[
            pltpu.SMEM((3, 4), i32), pltpu.SMEM((4,), i32), pltpu.SMEM((4, 8), i32),
            pltpu.VMEM((4, 8, 4096), f32), pltpu.VMEM((136, LANES), f32), pltpu.SemaphoreType.DMA((9,)),
        ],
        compiler_params=pltpu.CompilerParams(vmem_limit_bytes=60 * 1024 * 1024),
    )(box_offsets, species, channels, projectors, real, imag)
    ahead = lax.ppermute(both, "fft", [(i, (i + 24) % SLABS) for i in range(SLABS)])
    rows = [list(range(8 * x, 8 * x + 8)) for x in range(4)]
    got = lax.all_to_all(slices, "fft", split_axis=0, concat_axis=0, tiled=True, axis_index_groups=rows)
    turn = call(phase_body, (vector_potential,), (), shape(4, 128, LANES))
    got, ahead, turn = lax.optimization_barrier((got, ahead, turn))
    chips = [[2 * y, 2 * y + 1] for y in range(8)]
    gathered = lax.all_gather(got, "band", axis_index_groups=chips)
    corners = call(pick_body, (), (got,), shape(8, LANES, dtype=i32))
    passed = lax.ppermute(got, "fft", [(i, (i + 8) % SLABS) for i in range(SLABS)])
    shares = call(
        coef_body, (corners,), (gathered.reshape(2, 576, LANES), both, ahead, turn), shape(SLABS, 16, LANES),
        (pltpu.VMEM((640, LANES), f32), square),
    )
    shares, passed, both = lax.optimization_barrier((shares, passed, both))
    local, high, low = call(
        local_body, (vector_potential,), (both, pot, x_table, y_table, z_table),
        (shape(256, LANES), matrix, matrix),
    )
    passed = lax.all_gather(passed, "band", axis_index_groups=chips)
    got = exchange(shares, "fft")
    beta, table, boxes = call(
        merge_body, (), (gathered, passed, coupling),
        (shape(2, 576, LANES), shape(64, LANES), shape(8, LANES, dtype=i32)),
    )
    rest, moved, shares = call(
        rest_body, (vector_potential, boxes), (beta, table, got, turn, local, high, low),
        (shape(256, LANES), shape(256, LANES), shape(SLABS, 16, LANES)), (window, square),
    )
    got = exchange(shares, "fft")
    first, shares = call(
        first_body, (vector_potential, boxes), (beta, got, turn, rest, moved, high, low),
        (shape(256, LANES), shape(SLABS, 16, LANES)), (window, square),
    )
    got = exchange(shares, "fft")
    near = call(second_body, (vector_potential,), (first, pot, y_table, z_table), shape(256, LANES))
    new_real, new_imag, weighted = call(
        final_body, (occupation, boxes), (beta, table, got, turn, both, first, near),
        (shape(128, LANES), shape(128, LANES), shape(BANDS, 8, LANES)), (whole, window, square),
    )
    density = jnp.sum(exchange(weighted, "band"), axis=0).reshape(2, 4, LANES)
    grid = (1, 2, NY, NZ)
    return new_real.reshape(grid), new_imag.reshape(grid), density


def solution(mesh):
    placed = (
        P("band", "fft", None, None),
        P("band", "fft", None, None),
        P("fft", None, None),
        P(),
        P("band"),
        P("fft", None, None),
        P(None, "fft"),
        P("fft"),
        P("fft", None),
        P(),
    )
    return jax.shard_map(
        per_device,
        mesh=mesh,
        in_specs=placed,
        out_specs=(
            P("band", "fft", None, None),
            P("band", "fft", None, None),
            P("fft", "band", None),
        ),
        check_vma=False,
    )
```

```python
import functools
import math

import jax
import jax.numpy as jnp
import numpy as np
from jax import lax
from jax.experimental import pallas as pl
from jax.experimental.pallas import tpu as pltpu
from jax.sharding import PartitionSpec as P

NX = 64
NY = 64
NZ = 128
BOX = 16
NPROJ = 8
SLABS = 32
BANDS = 16
REACH = 9
KINDS = 4
LANES = 128
IMAG = 64

time_step = 0.01
kinetic_scale = 0.5 * (2.0 * math.pi / 38.0) ** 2
highest = lax.Precision.HIGHEST
f32 = jnp.float32
i32 = jnp.int32


def circulant(length):
    modes = np.arange(length)
    modes = np.where(modes < length // 2, modes, modes - length).astype(np.float64)
    steps = np.arange(length)
    wave = np.exp(2j * np.pi * np.outer(steps, modes) / length) / length
    apart = (steps[:, None] - steps[None, :]) % length
    return (wave @ modes**2)[apart] * kinetic_scale, (wave @ modes)[apart] * 2.0 * kinetic_scale


def blocks(matrix):
    return np.array([[matrix.real, -matrix.imag], [matrix.imag, matrix.real]])


def along_x(matrix):
    whole = blocks(matrix).reshape(2, 2, SLABS, 2, SLABS, 2)
    out = np.einsum("cdipjq,yz->iycpjzdq", whole, np.eye(2))
    return out.reshape(256, 256).astype(np.float32)


def along_y(matrix):
    out = np.einsum("cdyz,pq->cpydqz", blocks(matrix), np.eye(2))
    return out.reshape(256, 256).astype(np.float32)


def along_z(matrix):
    return np.einsum("cdyz->dzcy", blocks(matrix)).reshape(256, 256).astype(np.float32)


def tables():
    x2, x1 = circulant(NX)
    y2, y1 = circulant(NY)
    z2, z1 = circulant(NZ)
    return (
        np.stack([along_x(x2), along_x(x1)]),
        np.stack([along_y(y2), along_y(y1)]),
        np.stack([along_z(z2), along_z(z1)]),
    )


def halves(value):
    high = value.astype(jnp.bfloat16)
    low = (value - high.astype(f32)).astype(jnp.bfloat16)
    return high, low


def group_matrix():
    row = lax.broadcasted_iota(i32, (NPROJ, LANES), 0)
    lane = lax.broadcasted_iota(i32, (NPROJ, LANES), 1)
    return (lane // BOX == row).astype(f32)


def split_matrix(table_ref, shift, high_ref, low_ref):
    high_ref[...], low_ref[...] = halves(table_ref[0] + shift * table_ref[1])


def dot_split(left, right):
    dot = functools.partial(jnp.dot, preferred_element_type=f32)
    return dot(left[0], right[0]) + (dot(left[0], right[1]) + dot(left[1], right[0]))


def kinetic_yz(field, y_split, z_split, constant):
    along = dot_split([ref[...] for ref in y_split], halves(field))
    wide = jnp.concatenate([field[:128], field[128:]], axis=1)
    across = dot_split(halves(wide), [ref[...] for ref in z_split])
    across = jnp.concatenate([across[:, :128], across[:, 128:]], axis=0)
    return along + across + constant * field


def kinetic_x(field, high_ref, low_ref, shift_ref):
    return dot_split((high_ref[...], low_ref[...]), halves(field)) + shift_ref[0:1, :] * field


def pack_body(
    boxes_hbm, species_hbm, channels_hbm, proj_hbm, real_hbm, imag_hbm, out_ref, both_ref,
    boxes_ref, species_ref, channels_ref, proj_ref, rows_ref, done,
):
    place = lax.axis_index("fft") % 8
    core = lax.axis_index("band") % 2
    copies = [
        pltpu.make_async_copy(boxes_hbm, boxes_ref, done.at[0]),
        pltpu.make_async_copy(species_hbm, species_ref, done.at[1]),
        pltpu.make_async_copy(channels_hbm, channels_ref, done.at[2]),
    ]
    copies += [pltpu.make_async_copy(proj_hbm.at[atom], proj_ref.at[atom], done.at[3 + atom]) for atom in range(4)]
    copies += [
        pltpu.make_async_copy(real_hbm, both_ref.at[pl.ds(0, 128)], done.at[7]),
        pltpu.make_async_copy(imag_hbm, both_ref.at[pl.ds(128, 128)], done.at[8]),
    ]
    for copy in copies:
        copy.start()
    sub = lax.broadcasted_iota(i32, (NPROJ, LANES), 0)
    lane = lax.broadcasted_iota(i32, (NPROJ, LANES), 1)
    cell = lane % BOX
    group = lane // BOX
    skew = ((group + sub) & 7) * BOX + cell
    shift = (sub - group) & 7
    for copy in copies[:3]:
        copy.wait()
    facts = jnp.zeros((NPROJ, LANES), f32)
    for atom in range(4):
        for channel in range(NPROJ):
            here = (sub == channel) & (lane == atom)
            facts = jnp.where(here, channels_ref[atom, channel].astype(f32), facts)
        facts = jnp.where(lane == 4 + atom, species_ref[atom].astype(f32), facts)
        facts = jnp.where(lane == 8 + atom, boxes_ref[1, atom].astype(f32), facts)
        facts = jnp.where(lane == 12 + atom, boxes_ref[2, atom].astype(f32), facts)
        facts = jnp.where(lane == 16 + atom, ((boxes_ref[0, atom] & 1)).astype(f32), facts)
    for target in range(8):
        out_ref[target, 64:72, :] = facts
    for atom in range(4):
        copies[3 + atom].wait()
        last = shift * BOX + ((cell - boxes_ref[2, atom]) & (BOX - 1))
        for cut in range(BOX):
            start = pl.multiple_of((2 * cut + core) * LANES, LANES)
            tile = proj_ref[atom, :, pl.ds(start, LANES)]
            tile = jnp.take_along_axis(tile, skew, axis=1)
            tile = jnp.take_along_axis(tile, shift, axis=0)
            tile = jnp.take_along_axis(tile, last, axis=1)
            rows_ref[pl.ds(cut * 8, 8), :] = tile
            if cut == 0:
                rows_ref[pl.ds(128, 8), :] = tile
        odd = (boxes_ref[0, atom] & 1)
        for target in range(8):
            start = (2 * (target - place) - odd) & (BOX - 1)
            out_ref[target, pl.ds(atom * 16, 16), :] = rows_ref[pl.ds(pl.multiple_of(start * 8, 8), 16), :]
    for copy in copies[7:]:
        copy.wait()


def pick_body(got_ref, boxes_ref):
    place = lax.axis_index("fft") % 8
    lane = lax.broadcasted_iota(i32, (NPROJ, LANES), 1)
    sub = lax.broadcasted_iota(i32, (NPROJ, LANES), 0)
    found = jnp.zeros((NPROJ, LANES), f32)
    for slot in range(8):
        facts = got_ref[slot, 64:72, :]
        here = lane // 4 == slot
        for row, offset in enumerate((8, 12, 16)):
            found = jnp.where(here & (sub == row), pltpu.roll(facts, (4 * slot - offset) % LANES, 1), found)
    odd = found[2:3, :].astype(i32)
    far = (2 * place + sub - 2) < 2 * (lane // 4) + odd
    boxes_ref[...] = jnp.where(sub < 2, found.astype(i32), jnp.where(far, 320, 0))


def merge_body(here_ref, passed_ref, coupling_ref, proj_ref, table_ref, boxes_ref):
    place = lax.axis_index("fft") % 8
    lane = lax.broadcasted_iota(i32, (NPROJ, LANES), 1)
    sub = lax.broadcasted_iota(i32, (NPROJ, LANES), 0)
    zero = jnp.zeros((NPROJ, LANES), f32)
    gates, kind, first_y, first_z = zero, zero, zero, zero
    for slot in range(REACH):
        facts = zero

        @pl.when(slot <= place)
        def _():
            for half in range(2):
                proj_ref[half, pl.ds(slot * 64, 64), :] = here_ref[half, min(slot, 7), 0:64, :]
            boxes_ref[...] = here_ref[0, min(slot, 7), 64:72, :].astype(i32)

        @pl.when(slot > place)
        def _():
            for half in range(2):
                proj_ref[half, pl.ds(slot * 64, 64), :] = passed_ref[half, max(slot - 1, 0), 0:64, :]
            boxes_ref[...] = passed_ref[0, max(slot - 1, 0), 64:72, :].astype(i32)

        facts = boxes_ref[...].astype(f32)
        here = lane // 4 == slot

        def moved(offset):
            return jnp.where(here, pltpu.roll(facts, (4 * slot - offset) % LANES, 1), 0.0)

        gates += moved(0)
        kind += moved(4)
        first_y += moved(8)
        first_z += moved(12)
    for behind in range(2):
        source = (here_ref, passed_ref)[behind]
        odds = source[0, place, 64:72, :]
        for atom in range(4):
            odd = odds[0:1, 16 + atom : 17 + atom]
            keep = (odd < 0.5) if behind == 0 else (odd > 0.5)
            start = pl.multiple_of((place + behind) * 64 + atom * 16, 16)
            for half in range(2):
                rows = proj_ref[half, pl.ds(start, 8), :]
                proj_ref[half, pl.ds(start, 8), :] = jnp.where(keep, rows, 0.0)
                if behind == 1:
                    proj_ref[half, pl.ds(start + 8, 8), :] = zero
    gates += pltpu.roll(gates, IMAG, 1)
    kind += pltpu.roll(kind, IMAG, 1)
    for other in range(NPROJ):
        value = zero
        for which in range(KINDS):
            column = coupling_ref[which][:, other : other + 1]
            value = jnp.where(kind == float(which), column, value)
        table_ref[pl.ds(other * 8, 8), :] = value * gates * gates[other : other + 1, :]
    boxes_ref[...] = jnp.where(sub == 0, first_y, first_z).astype(i32)


def phase_body(vector_ref, occupation_ref, turn_ref, shift_ref):
    slab = lax.axis_index("fft")
    row = lax.broadcasted_iota(i32, (128, LANES), 0)
    y = (row % NY).astype(f32)
    z = lax.broadcasted_iota(i32, (128, LANES), 1).astype(f32)
    for ahead in range(2):
        x = ((slab + 8 * ahead) % SLABS * 2 + row // NY).astype(f32)
        turns = vector_ref[0] * x / NX + vector_ref[1] * y / NY + vector_ref[2] * z / NZ
        turns = turns - jnp.floor(turns + 0.5)
        theta = (2.0 * math.pi) * turns
        turn_ref[2 * ahead] = jnp.cos(theta)
        turn_ref[2 * ahead + 1] = jnp.sin(theta)
    squares = [kinetic_scale * vector_ref[axis] * vector_ref[axis] for axis in range(3)]
    sub = lax.broadcasted_iota(i32, (8, LANES), 0)
    rows = jnp.where(sub == 1, occupation_ref[0], squares[1] + squares[2])
    shift_ref[...] = jnp.where(sub == 0, squares[0], rows)


def local_body(vector_ref, both_ref, pot_ref, x_ref, y_ref, z_ref, out_ref, *split_refs):
    for axis, table_ref in enumerate((x_ref, y_ref, z_ref)):
        split_matrix(table_ref, vector_ref[axis], split_refs[2 * axis], split_refs[2 * axis + 1])
    field = both_ref[...]
    constant = kinetic_scale * (vector_ref[1] * vector_ref[1] + vector_ref[2] * vector_ref[2])
    out = kinetic_yz(field, split_refs[2:4], split_refs[4:6], constant)
    pot = pot_ref[...]
    out_ref[...] = out + jnp.concatenate([pot, pot], axis=0) * field


def turned_rows(real, imag, cosine, sine, field_ref, first_row):
    turned = (cosine * real - sine * imag, sine * real + cosine * imag)
    for part in range(2):
        for plane in range(2):
            base = first_row + (part * 2 + plane) * 80
            field_ref[pl.ds(base, 64), :] = turned[part][plane * 64 : plane * 64 + 64]
            field_ref[pl.ds(base + 64, 16), :] = turned[part][plane * 64 : plane * 64 + 16]


def project(boxes_ref, proj_ref, wide, far, atoms, field_ref, sums_ref):
    sums_ref[...] = jnp.zeros_like(sums_ref)
    cell = lax.broadcasted_iota(i32, (BOX, LANES), 1) % BOX

    def one(atom, carry):
        first_y = boxes_ref[0, atom]
        first_z = boxes_ref[1, atom]
        pick = (first_z + ((cell - first_z) & (BOX - 1))) & (LANES - 1)
        total = [None, None]
        for plane in range(2):
            start = pl.multiple_of(atom // 4 * wide + atom % 4 * 16 + plane * 8, 8)
            beta = jnp.concatenate([proj_ref[0, pl.ds(start, 8), :], proj_ref[1, pl.ds(start, 8), :]], axis=0)
            base = first_y + boxes_ref[2 + plane, atom] if far else first_y
            for part in range(2):
                rows = field_ref[pl.ds((part * 2 + plane) * 80 + base, BOX), :]
                term = beta * jnp.take_along_axis(rows, pick, axis=1)
                total[part] = term if plane == 0 else total[part] + term
        for part in range(2):
            sums_ref[pl.ds(part * IMAG + atom, 1), :] = jnp.sum(total[part], axis=0, keepdims=True)
        return carry

    lax.fori_loop(0, atoms, one, 0, unroll=True)
    return lax.dot_general(
        group_matrix(), sums_ref[...], (((1,), (1,)), ((), ())), precision=highest, preferred_element_type=f32
    )


def row_sums(got_ref, row, kept):
    total = jnp.zeros((NPROJ, LANES), f32)
    for place in range(8):
        share = got_ref[row % 4 * 8 + place, 8:16, :]
        total += share if kept is None else jnp.where(kept(place), share, 0.0)
    return total


def first_coefs(slab, got_ref):
    group = lax.broadcasted_iota(i32, (NPROJ, LANES), 1) % IMAG // 4
    own = row_sums(got_ref, slab // 8, None)
    before = row_sums(got_ref, slab // 8 + 3, None)
    return jnp.where(group <= slab % 8, own, pltpu.roll(before, 4, 1))


def second_coefs(slab, got_ref):
    group = lax.broadcasted_iota(i32, (NPROJ, LANES), 1) % IMAG // 4
    row = slab // 8

    def own(place):
        return group <= place

    def passed(place):
        return (group > place) & (group < REACH)

    here = row_sums(got_ref, row, own) + pltpu.roll(row_sums(got_ref, row + 1, passed), LANES - 4, 1)
    before = pltpu.roll(row_sums(got_ref, row + 3, own), 4, 1) + row_sums(got_ref, row, passed)
    return jnp.where(group <= slab % 8, here, jnp.where(group < REACH, before, 0.0))


def spread(coef, boxes_ref, proj_ref, table_ref, turn_ref, place_ref, dual_ref):
    dual = jnp.zeros((NPROJ, LANES), f32)
    for other in range(NPROJ):
        dual += table_ref[pl.ds(other * 8, 8), :] * coef[other : other + 1, :]
    dual_ref[...] = lax.dot_general(
        dual, group_matrix(), (((0,), (0,)), ((), ())), precision=highest, preferred_element_type=f32
    )
    place_ref[...] = jnp.zeros_like(place_ref)
    left = lax.broadcasted_iota(i32, (256, 256), 0)
    right = lax.broadcasted_iota(i32, (256, 256), 1)
    gather = ((left // LANES == right // LANES) & (left % BOX == right % BOX)).astype(f32).astype(jnp.bfloat16)
    wide = lax.broadcasted_iota(i32, (8, 2 * LANES), 1) % LANES
    dot = functools.partial(jnp.dot, preferred_element_type=f32)
    for distance in range(REACH):
        rows = []
        for half in range(2):
            for atom in range(4 * distance, 4 * distance + 4):
                beta = proj_ref[half, pl.ds(atom * 16, 16), :]
                real = beta * dual_ref[pl.ds(atom, 1), :]
                imag = beta * dual_ref[pl.ds(IMAG + atom, 1), :]
                rows.append(jnp.concatenate([real, imag], axis=1))
        high, low = halves(jnp.concatenate(rows, axis=0))
        value = dot(high, gather) + dot(low, gather)
        for atom in range(4 * distance, 4 * distance + 4):
            first_y = boxes_ref[0, atom]
            first_z = boxes_ref[1, atom]
            inside = ((wide - first_z) & (LANES - 1)) < BOX
            for plane in range(2):
                parts = []
                for half in range(2):
                    start = half * 64 + (atom % 4) * 16 + plane * 8
                    parts.append(jnp.where(inside, value[start : start + 8], 0.0))
                both = jnp.concatenate(parts, axis=0)
                place_ref[pl.ds(plane * 80 + first_y, BOX), :] += both[:, :LANES]
                place_ref[pl.ds(160 + plane * 80 + first_y, BOX), :] += both[:, LANES:]
    for block in range(4):
        place_ref[pl.ds(block * 80, 16), :] += place_ref[pl.ds(block * 80 + 64, 16), :]
    back_real = jnp.concatenate([place_ref[pl.ds(0, 64), :], place_ref[pl.ds(80, 64), :]], axis=0)
    back_imag = jnp.concatenate([place_ref[pl.ds(160, 64), :], place_ref[pl.ds(240, 64), :]], axis=0)
    cosine, sine = turn_ref[0], turn_ref[1]
    return cosine * back_real + sine * back_imag, cosine * back_imag - sine * back_real


def columns(field_ref, out_ref):
    for y in range(2):
        for part in range(2):
            for plane in range(2):
                row = y * 4 + part * 2 + plane
                start = part * 128 + plane * 64 + y
                out_ref[:, row, :] = field_ref[pl.ds(start, SLABS, stride=2), :]


def unpack(got_ref, first_row, field_ref):
    for y in range(2):
        for part in range(2):
            for plane in range(2):
                row = y * 4 + part * 2 + plane
                start = part * 128 + plane * 64 + y
                field_ref[pl.ds(start, SLABS, stride=2), :] = got_ref[:, first_row + row, :]


def fetch(source_ref, boxes_ref, done):
    copy = pltpu.make_async_copy(source_ref, boxes_ref, done.at[0])
    copy.start()
    return copy


def coef_body(
    corner_ref, proj_ref, both_ref, next_ref, turn_ref, out_ref, field_ref, sums_ref, boxes_ref, done
):
    copy = fetch(corner_ref, boxes_ref, done)
    columns(both_ref, out_ref)
    for ahead, ref in enumerate((both_ref, next_ref)):
        turned_rows(
            ref[0:128, :], ref[128:256, :], turn_ref[2 * ahead], turn_ref[2 * ahead + 1], field_ref, 320 * ahead
        )
    copy.wait()
    coef = project(boxes_ref, proj_ref, 72, True, 32, field_ref, sums_ref)
    out_ref[:, 8:16, :] = jnp.broadcast_to(coef[None], (SLABS, 8, LANES))


def rest_body(
    corner_ref, shift_ref, proj_ref, table_ref, got_ref, turn_ref, local_ref, high_ref, low_ref,
    rest_ref, moved_ref, out_ref, place_ref, dual_ref, boxes_ref, done,
):
    copy = fetch(corner_ref, boxes_ref, done)
    field = got_ref[:, 0:8, :].reshape(256, LANES)
    moved = kinetic_x(field, high_ref, low_ref, shift_ref)
    moved_ref[...] = moved
    out_ref[:, 8:16, :] = moved.reshape(SLABS, 8, LANES)
    coef = first_coefs(lax.axis_index("fft"), got_ref)
    copy.wait()
    far_real, far_imag = spread(coef, boxes_ref, proj_ref, table_ref, turn_ref, place_ref, dual_ref)
    rest_ref[0:128, :] = local_ref[0:128, :] + far_real
    rest_ref[128:256, :] = local_ref[128:256, :] + far_imag
    columns(rest_ref, out_ref)


def first_body(
    corner_ref, shift_ref, proj_ref, got_ref, turn_ref, rest_ref, moved_ref, high_ref, low_ref,
    first_ref, out_ref, field_ref, sums_ref, boxes_ref, done,
):
    copy = fetch(corner_ref, boxes_ref, done)
    field = got_ref[:, 0:8, :].reshape(256, LANES) + moved_ref[...]
    out_ref[:, 0:8, :] = kinetic_x(field, high_ref, low_ref, shift_ref).reshape(SLABS, 8, LANES)
    unpack(got_ref, 8, first_ref)
    real = first_ref[0:128, :] + rest_ref[0:128, :]
    imag = first_ref[128:256, :] + rest_ref[128:256, :]
    first_ref[0:128, :] = real
    first_ref[128:256, :] = imag
    turned_rows(real, imag, turn_ref[0], turn_ref[1], field_ref, 0)
    copy.wait()
    coef = project(boxes_ref, proj_ref, 64, False, 4 * REACH, field_ref, sums_ref)
    out_ref[:, 8:16, :] = jnp.broadcast_to(coef[None], (SLABS, 8, LANES))


def final_body(
    corner_ref, shift_ref, proj_ref, table_ref, got_ref, turn_ref, both_ref, first_ref, pot_ref,
    y_high_ref, y_low_ref, z_high_ref, z_low_ref,
    new_real_ref, new_imag_ref, out_ref, field_ref, place_ref, dual_ref, boxes_ref, done,
):
    copy = fetch(corner_ref, boxes_ref, done)
    unpack(got_ref, 0, field_ref)
    coef = second_coefs(lax.axis_index("fft"), got_ref)
    copy.wait()
    far_real, far_imag = spread(coef, boxes_ref, proj_ref, table_ref, turn_ref, place_ref, dual_ref)
    half = 0.5 * time_step * time_step
    first = first_ref[...]
    near = kinetic_yz(first, (y_high_ref, y_low_ref), (z_high_ref, z_low_ref), shift_ref[2:3, :])
    pot = pot_ref[...]
    second_real = near[:128] + pot * first[:128] + field_ref[0:128, :] + far_real
    second_imag = near[128:] + pot * first[128:] + field_ref[128:256, :] + far_imag
    new_real = both_ref[0:128, :] + time_step * first_ref[128:256, :] - half * second_real
    new_imag = both_ref[128:256, :] - time_step * first_ref[0:128, :] - half * second_imag
    new_real_ref[...] = new_real
    new_imag_ref[...] = new_imag
    weighted = shift_ref[1:2, :] * (new_real * new_real + new_imag * new_imag)
    weighted = weighted.reshape(2, BANDS, 4, LANES)
    for plane in range(2):
        out_ref[:, pl.ds(plane * 4, 4), :] = weighted[plane]


def smem():
    return pl.BlockSpec(memory_space=pltpu.SMEM)


def vmem():
    return pl.BlockSpec(memory_space=pltpu.VMEM)


def call(body, scalars, arrays, outs, scratch=(), cost=None):
    several = isinstance(outs, tuple)
    return pl.pallas_call(
        body,
        out_shape=outs,
        in_specs=[smem()] * len(scalars) + [vmem()] * len(arrays),
        out_specs=tuple(vmem() for _ in outs) if several else vmem(),
        scratch_shapes=list(scratch),
        compiler_params=pltpu.CompilerParams(vmem_limit_bytes=24 * 1024 * 1024),
        cost_estimate=cost,
    )(*scalars, *arrays)


def shape(*dims, dtype=f32):
    return jax.ShapeDtypeStruct(dims, dtype)


def exchange(value, axis):
    return lax.all_to_all(value, axis, split_axis=0, concat_axis=0, tiled=True)


def per_device(
    psi_real, psi_imag, potential, vector_potential, occupation, projectors, box_offsets, species, channels, coupling
):
    x_table, y_table, z_table = (jnp.asarray(table) for table in tables())
    real = psi_real.reshape(128, LANES)
    imag = psi_imag.reshape(128, LANES)
    pot = potential.reshape(128, LANES)
    matrix = jax.ShapeDtypeStruct((256, 256), jnp.bfloat16)
    corner = pltpu.SMEM((8, LANES), i32)
    signal = pltpu.SemaphoreType.DMA((1,))
    window = pltpu.VMEM((320, LANES), f32)
    square = pltpu.VMEM((128, LANES), f32)
    whole = pltpu.VMEM((256, LANES), f32)

    anywhere = pl.BlockSpec(memory_space=pltpu.HBM)
    slices, both = pl.pallas_call(
        pack_body,
        out_shape=(shape(8, 72, LANES), shape(256, LANES)),
        in_specs=[anywhere] * 6,
        out_specs=(vmem(), vmem()),
        scratch_shapes=[
            pltpu.SMEM((3, 4), i32), pltpu.SMEM((4,), i32), pltpu.SMEM((4, 8), i32),
            pltpu.VMEM((4, 8, 4096), f32), pltpu.VMEM((136, LANES), f32), pltpu.SemaphoreType.DMA((9,)),
        ],
        compiler_params=pltpu.CompilerParams(vmem_limit_bytes=60 * 1024 * 1024),
    )(box_offsets, species, channels, projectors, real, imag)
    ahead = lax.ppermute(both, "fft", [(i, (i + 24) % SLABS) for i in range(SLABS)])
    rows = [list(range(8 * x, 8 * x + 8)) for x in range(4)]
    got = lax.all_to_all(slices, "fft", split_axis=0, concat_axis=0, tiled=True, axis_index_groups=rows)
    turn, shift = call(phase_body, (vector_potential, occupation), (), (shape(4, 128, LANES), shape(8, LANES)))
    got, ahead, turn, shift = lax.optimization_barrier((got, ahead, turn, shift))
    chips = [[2 * y, 2 * y + 1] for y in range(8)]
    gathered = lax.all_gather(got, "band", axis_index_groups=chips)
    corners = call(pick_body, (), (got,), shape(8, LANES, dtype=i32))
    passed = lax.ppermute(got, "fft", [(i, (i + 8) % SLABS) for i in range(SLABS)])
    shares = call(
        coef_body, (), (corners, gathered.reshape(2, 576, LANES), both, ahead, turn), shape(SLABS, 16, LANES),
        (pltpu.VMEM((640, LANES), f32), square, corner, signal),
    )
    shares, passed, both = lax.optimization_barrier((shares, passed, both))
    local, high, low, *yz_split = call(
        local_body, (vector_potential,), (both, pot, x_table, y_table, z_table),
        (shape(256, LANES),) + (matrix,) * 6,
    )
    passed = lax.all_gather(passed, "band", axis_index_groups=chips)
    got = exchange(shares, "fft")
    beta, table, boxes = call(
        merge_body, (), (gathered, passed, coupling),
        (shape(2, 576, LANES), shape(64, LANES), shape(8, LANES, dtype=i32)),
    )
    rest, moved, shares = call(
        rest_body, (), (boxes, shift, beta, table, got, turn, local, high, low),
        (shape(256, LANES), shape(256, LANES), shape(SLABS, 16, LANES)), (window, square, corner, signal),
    )
    got = exchange(shares, "fft")
    first, shares = call(
        first_body, (), (boxes, shift, beta, got, turn, rest, moved, high, low),
        (shape(256, LANES), shape(SLABS, 16, LANES)), (window, square, corner, signal),
    )
    got = exchange(shares, "fft")
    new_real, new_imag, weighted = call(
        final_body, (), (boxes, shift, beta, table, got, turn, both, first, pot, *yz_split),
        (shape(128, LANES), shape(128, LANES), shape(BANDS, 8, LANES)), (whole, window, square, corner, signal),
    )
    density = jnp.sum(exchange(weighted, "band"), axis=0).reshape(2, 4, LANES)
    grid = (1, 2, NY, NZ)
    return new_real.reshape(grid), new_imag.reshape(grid), density


def solution(mesh):
    placed = (
        P("band", "fft", None, None),
        P("band", "fft", None, None),
        P("fft", None, None),
        P(),
        P("band"),
        P("fft", None, None),
        P(None, "fft"),
        P("fft"),
        P("fft", None),
        P(),
    )
    return jax.shard_map(
        per_device,
        mesh=mesh,
        in_specs=placed,
        out_specs=(
            P("band", "fft", None, None),
            P("band", "fft", None, None),
            P("fft", "band", None),
        ),
        check_vma=False,
    )
```

```python
import functools
import math

import jax
import jax.numpy as jnp
import numpy as np
from jax import lax
from jax.experimental import pallas as pl
from jax.experimental.pallas import tpu as pltpu
from jax.sharding import PartitionSpec as P

NX = 64
NY = 64
NZ = 128
BOX = 16
NPROJ = 8
SLABS = 32
BANDS = 16
REACH = 9
KINDS = 4
LANES = 128
IMAG = 64

time_step = 0.01
kinetic_scale = 0.5 * (2.0 * math.pi / 38.0) ** 2
highest = lax.Precision.HIGHEST
f32 = jnp.float32
i32 = jnp.int32


def circulant(length):
    modes = np.arange(length)
    modes = np.where(modes < length // 2, modes, modes - length).astype(np.float64)
    steps = np.arange(length)
    wave = np.exp(2j * np.pi * np.outer(steps, modes) / length) / length
    apart = (steps[:, None] - steps[None, :]) % length
    return (wave @ modes**2)[apart] * kinetic_scale, (wave @ modes)[apart] * 2.0 * kinetic_scale


def blocks(matrix):
    return np.array([[matrix.real, -matrix.imag], [matrix.imag, matrix.real]])


def along_x(matrix):
    whole = blocks(matrix).reshape(2, 2, SLABS, 2, SLABS, 2)
    out = np.einsum("cdipjq,yz->iycpjzdq", whole, np.eye(2))
    return out.reshape(256, 256).astype(np.float32)


def along_y(matrix):
    out = np.einsum("cdyz,pq->cpydqz", blocks(matrix), np.eye(2))
    return out.reshape(256, 256).astype(np.float32)


def along_z(matrix):
    return np.einsum("cdyz->dzcy", blocks(matrix)).reshape(256, 256).astype(np.float32)


def tables():
    x2, x1 = circulant(NX)
    y2, y1 = circulant(NY)
    z2, z1 = circulant(NZ)
    return (
        np.stack([along_x(x2), along_x(x1)]),
        np.stack([along_y(y2), along_y(y1)]),
        np.stack([along_z(z2), along_z(z1)]),
    )


def halves(value):
    high = value.astype(jnp.bfloat16)
    low = (value - high.astype(f32)).astype(jnp.bfloat16)
    return high, low


def group_matrix():
    row = lax.broadcasted_iota(i32, (NPROJ, LANES), 0)
    lane = lax.broadcasted_iota(i32, (NPROJ, LANES), 1)
    return (lane // BOX == row).astype(f32)


def split_matrix(table_ref, shift, high_ref, low_ref):
    high_ref[...], low_ref[...] = halves(table_ref[0] + shift * table_ref[1])


def dot_split(left, right):
    dot = functools.partial(jnp.dot, preferred_element_type=f32)
    return dot(left[0], right[0]) + (dot(left[0], right[1]) + dot(left[1], right[0]))


def kinetic_yz(field, y_split, z_split, constant):
    along = dot_split([ref[...] for ref in y_split], halves(field))
    wide = jnp.concatenate([field[:128], field[128:]], axis=1)
    across = dot_split(halves(wide), [ref[...] for ref in z_split])
    across = jnp.concatenate([across[:, :128], across[:, 128:]], axis=0)
    return along + across + constant * field


def kinetic_x(field, high_ref, low_ref, shift_ref):
    return dot_split((high_ref[...], low_ref[...]), halves(field)) + shift_ref[0:1, :] * field


def pack_body(
    boxes_hbm, species_hbm, channels_hbm, proj_hbm, real_hbm, imag_hbm, out_ref, both_ref,
    boxes_ref, species_ref, channels_ref, proj_ref, rows_ref, done,
):
    place = lax.axis_index("fft") % 8
    core = lax.axis_index("band") % 2
    copies = [
        pltpu.make_async_copy(boxes_hbm, boxes_ref, done.at[0]),
        pltpu.make_async_copy(species_hbm, species_ref, done.at[1]),
        pltpu.make_async_copy(channels_hbm, channels_ref, done.at[2]),
    ]
    copies += [pltpu.make_async_copy(proj_hbm.at[atom], proj_ref.at[atom], done.at[3 + atom]) for atom in range(4)]
    copies += [
        pltpu.make_async_copy(real_hbm, both_ref.at[pl.ds(0, 128)], done.at[7]),
        pltpu.make_async_copy(imag_hbm, both_ref.at[pl.ds(128, 128)], done.at[8]),
    ]
    for copy in copies:
        copy.start()
    sub = lax.broadcasted_iota(i32, (NPROJ, LANES), 0)
    lane = lax.broadcasted_iota(i32, (NPROJ, LANES), 1)
    cell = lane % BOX
    group = lane // BOX
    skew = ((group + sub) & 7) * BOX + cell
    shift = (sub - group) & 7
    for copy in copies[:3]:
        copy.wait()
    facts = jnp.zeros((NPROJ, LANES), f32)
    for atom in range(4):
        for channel in range(NPROJ):
            here = (sub == channel) & (lane == atom)
            facts = jnp.where(here, channels_ref[atom, channel].astype(f32), facts)
        facts = jnp.where(lane == 4 + atom, species_ref[atom].astype(f32), facts)
        facts = jnp.where(lane == 8 + atom, boxes_ref[1, atom].astype(f32), facts)
        facts = jnp.where(lane == 12 + atom, boxes_ref[2, atom].astype(f32), facts)
        facts = jnp.where(lane == 16 + atom, ((boxes_ref[0, atom] & 1)).astype(f32), facts)
    for target in range(8):
        out_ref[target, 64:72, :] = facts
    for atom in range(4):
        copies[3 + atom].wait()
        last = shift * BOX + ((cell - boxes_ref[2, atom]) & (BOX - 1))
        for cut in range(BOX):
            start = pl.multiple_of((2 * cut + core) * LANES, LANES)
            tile = proj_ref[atom, :, pl.ds(start, LANES)]
            tile = jnp.take_along_axis(tile, skew, axis=1)
            tile = jnp.take_along_axis(tile, shift, axis=0)
            tile = jnp.take_along_axis(tile, last, axis=1)
            rows_ref[pl.ds(cut * 8, 8), :] = tile
            if cut == 0:
                rows_ref[pl.ds(128, 8), :] = tile
        odd = (boxes_ref[0, atom] & 1)
        for target in range(8):
            start = (2 * (target - place) - odd) & (BOX - 1)
            out_ref[target, pl.ds(atom * 16, 16), :] = rows_ref[pl.ds(pl.multiple_of(start * 8, 8), 16), :]
    for copy in copies[7:]:
        copy.wait()


def pick_body(got_ref, boxes_ref):
    place = lax.axis_index("fft") % 8
    lane = lax.broadcasted_iota(i32, (NPROJ, LANES), 1)
    sub = lax.broadcasted_iota(i32, (NPROJ, LANES), 0)
    found = jnp.zeros((NPROJ, LANES), f32)
    for slot in range(8):
        facts = got_ref[slot, 64:72, :]
        here = lane // 4 == slot
        for row, offset in enumerate((8, 12, 16)):
            found = jnp.where(here & (sub == row), pltpu.roll(facts, (4 * slot - offset) % LANES, 1), found)
    odd = found[2:3, :].astype(i32)
    far = (2 * place + sub - 2) < 2 * (lane // 4) + odd
    boxes_ref[...] = jnp.where(sub < 2, found.astype(i32), jnp.where(far, 320, 0))


def merge_body(here_ref, passed_ref, coupling_ref, proj_ref, table_ref, boxes_ref):
    place = lax.axis_index("fft") % 8
    lane = lax.broadcasted_iota(i32, (NPROJ, LANES), 1)
    sub = lax.broadcasted_iota(i32, (NPROJ, LANES), 0)
    zero = jnp.zeros((NPROJ, LANES), f32)
    gates, kind, first_y, first_z = zero, zero, zero, zero
    for slot in range(REACH):
        facts = zero

        @pl.when(slot <= place)
        def _():
            for half in range(2):
                proj_ref[half, pl.ds(slot * 64, 64), :] = here_ref[half, min(slot, 7), 0:64, :]
            boxes_ref[...] = here_ref[0, min(slot, 7), 64:72, :].astype(i32)

        @pl.when(slot > place)
        def _():
            for half in range(2):
                proj_ref[half, pl.ds(slot * 64, 64), :] = passed_ref[half, max(slot - 1, 0), 0:64, :]
            boxes_ref[...] = passed_ref[0, max(slot - 1, 0), 64:72, :].astype(i32)

        facts = boxes_ref[...].astype(f32)
        here = lane // 4 == slot

        def moved(offset):
            return jnp.where(here, pltpu.roll(facts, (4 * slot - offset) % LANES, 1), 0.0)

        gates += moved(0)
        kind += moved(4)
        first_y += moved(8)
        first_z += moved(12)
    for behind in range(2):
        source = (here_ref, passed_ref)[behind]
        odds = source[0, place, 64:72, :]
        for atom in range(4):
            odd = odds[0:1, 16 + atom : 17 + atom]
            keep = (odd < 0.5) if behind == 0 else (odd > 0.5)
            start = pl.multiple_of((place + behind) * 64 + atom * 16, 16)
            for half in range(2):
                rows = proj_ref[half, pl.ds(start, 8), :]
                proj_ref[half, pl.ds(start, 8), :] = jnp.where(keep, rows, 0.0)
                if behind == 1:
                    proj_ref[half, pl.ds(start + 8, 8), :] = zero
    gates += pltpu.roll(gates, IMAG, 1)
    kind += pltpu.roll(kind, IMAG, 1)
    for other in range(NPROJ):
        value = zero
        for which in range(KINDS):
            column = coupling_ref[which][:, other : other + 1]
            value = jnp.where(kind == float(which), column, value)
        table_ref[pl.ds(other * 8, 8), :] = value * gates * gates[other : other + 1, :]
    boxes_ref[...] = jnp.where(sub == 0, first_y, first_z).astype(i32)


def phase_body(vector_ref, occupation_ref, turn_ref, shift_ref):
    slab = lax.axis_index("fft")
    row = lax.broadcasted_iota(i32, (128, LANES), 0)
    y = (row % NY).astype(f32)
    z = lax.broadcasted_iota(i32, (128, LANES), 1).astype(f32)
    for ahead in range(2):
        x = ((slab + 8 * ahead) % SLABS * 2 + row // NY).astype(f32)
        turns = vector_ref[0] * x / NX + vector_ref[1] * y / NY + vector_ref[2] * z / NZ
        turns = turns - jnp.floor(turns + 0.5)
        theta = (2.0 * math.pi) * turns
        turn_ref[2 * ahead] = jnp.cos(theta)
        turn_ref[2 * ahead + 1] = jnp.sin(theta)
    squares = [kinetic_scale * vector_ref[axis] * vector_ref[axis] for axis in range(3)]
    sub = lax.broadcasted_iota(i32, (8, LANES), 0)
    rows = jnp.where(sub == 1, occupation_ref[0], squares[1] + squares[2])
    shift_ref[...] = jnp.where(sub == 0, squares[0], rows)


def local_body(vector_ref, both_ref, pot_ref, x_ref, y_ref, z_ref, out_ref, *split_refs):
    for axis, table_ref in enumerate((x_ref, y_ref, z_ref)):
        split_matrix(table_ref, vector_ref[axis], split_refs[2 * axis], split_refs[2 * axis + 1])
    field = both_ref[...]
    constant = kinetic_scale * (vector_ref[1] * vector_ref[1] + vector_ref[2] * vector_ref[2])
    out = kinetic_yz(field, split_refs[2:4], split_refs[4:6], constant)
    pot = pot_ref[...]
    out_ref[...] = out + jnp.concatenate([pot, pot], axis=0) * field


def turned_rows(real, imag, cosine, sine, field_ref, first_row):
    turned = (cosine * real - sine * imag, sine * real + cosine * imag)
    for part in range(2):
        for plane in range(2):
            base = first_row + (part * 2 + plane) * 80
            field_ref[pl.ds(base, 64), :] = turned[part][plane * 64 : plane * 64 + 64]
            field_ref[pl.ds(base + 64, 16), :] = turned[part][plane * 64 : plane * 64 + 16]


def project(boxes_ref, proj_ref, wide, far, atoms, field_ref, sums_ref):
    sums_ref[...] = jnp.zeros_like(sums_ref)
    cell = lax.broadcasted_iota(i32, (BOX, LANES), 1) % BOX

    def one(atom, carry):
        first_y = boxes_ref[0, atom]
        first_z = boxes_ref[1, atom]
        pick = (first_z + ((cell - first_z) & (BOX - 1))) & (LANES - 1)
        total = [None, None]
        for plane in range(2):
            start = pl.multiple_of(atom // 4 * wide + atom % 4 * 16 + plane * 8, 8)
            beta = jnp.concatenate([proj_ref[0, pl.ds(start, 8), :], proj_ref[1, pl.ds(start, 8), :]], axis=0)
            base = first_y + boxes_ref[2 + plane, atom] if far else first_y
            for part in range(2):
                rows = field_ref[pl.ds((part * 2 + plane) * 80 + base, BOX), :]
                term = beta * jnp.take_along_axis(rows, pick, axis=1)
                total[part] = term if plane == 0 else total[part] + term
        for part in range(2):
            sums_ref[pl.ds(part * IMAG + atom, 1), :] = jnp.sum(total[part], axis=0, keepdims=True)
        return carry

    lax.fori_loop(0, atoms, one, 0, unroll=True)
    return lax.dot_general(
        group_matrix(), sums_ref[...], (((1,), (1,)), ((), ())), precision=highest, preferred_element_type=f32
    )


def row_sums(got_ref, row, kept):
    total = jnp.zeros((NPROJ, LANES), f32)
    for place in range(8):
        share = got_ref[row % 4 * 8 + place, 8:16, :]
        total += share if kept is None else jnp.where(kept(place), share, 0.0)
    return total


def first_coefs(slab, got_ref):
    group = lax.broadcasted_iota(i32, (NPROJ, LANES), 1) % IMAG // 4
    own = row_sums(got_ref, slab // 8, None)
    before = row_sums(got_ref, slab // 8 + 3, None)
    return jnp.where(group <= slab % 8, own, pltpu.roll(before, 4, 1))


def second_coefs(slab, got_ref):
    group = lax.broadcasted_iota(i32, (NPROJ, LANES), 1) % IMAG // 4
    row = slab // 8

    def own(place):
        return group <= place

    def passed(place):
        return (group > place) & (group < REACH)

    here = row_sums(got_ref, row, own) + pltpu.roll(row_sums(got_ref, row + 1, passed), LANES - 4, 1)
    before = pltpu.roll(row_sums(got_ref, row + 3, own), 4, 1) + row_sums(got_ref, row, passed)
    return jnp.where(group <= slab % 8, here, jnp.where(group < REACH, before, 0.0))


def spread(coef, boxes_ref, proj_ref, table_ref, turn_ref, place_ref, dual_ref):
    dual = jnp.zeros((NPROJ, LANES), f32)
    for other in range(NPROJ):
        dual += table_ref[pl.ds(other * 8, 8), :] * coef[other : other + 1, :]
    dual_ref[...] = lax.dot_general(
        dual, group_matrix(), (((0,), (0,)), ((), ())), precision=highest, preferred_element_type=f32
    )
    place_ref[...] = jnp.zeros_like(place_ref)
    left = lax.broadcasted_iota(i32, (256, 256), 0)
    right = lax.broadcasted_iota(i32, (256, 256), 1)
    gather = ((left // LANES == right // LANES) & (left % BOX == right % BOX)).astype(f32).astype(jnp.bfloat16)
    wide = lax.broadcasted_iota(i32, (8, 2 * LANES), 1) % LANES
    dot = functools.partial(jnp.dot, preferred_element_type=f32)
    for distance in range(REACH):
        rows = []
        for half in range(2):
            for atom in range(4 * distance, 4 * distance + 4):
                beta = proj_ref[half, pl.ds(atom * 16, 16), :]
                real = beta * dual_ref[pl.ds(atom, 1), :]
                imag = beta * dual_ref[pl.ds(IMAG + atom, 1), :]
                rows.append(jnp.concatenate([real, imag], axis=1))
        high, low = halves(jnp.concatenate(rows, axis=0))
        value = dot(high, gather) + dot(low, gather)
        for atom in range(4 * distance, 4 * distance + 4):
            first_y = boxes_ref[0, atom]
            first_z = boxes_ref[1, atom]
            inside = ((wide - first_z) & (LANES - 1)) < BOX
            for plane in range(2):
                parts = []
                for half in range(2):
                    start = half * 64 + (atom % 4) * 16 + plane * 8
                    parts.append(jnp.where(inside, value[start : start + 8], 0.0))
                both = jnp.concatenate(parts, axis=0)
                place_ref[pl.ds(plane * 80 + first_y, BOX), :] += both[:, :LANES]
                place_ref[pl.ds(160 + plane * 80 + first_y, BOX), :] += both[:, LANES:]
    for block in range(4):
        place_ref[pl.ds(block * 80, 16), :] += place_ref[pl.ds(block * 80 + 64, 16), :]
    back_real = jnp.concatenate([place_ref[pl.ds(0, 64), :], place_ref[pl.ds(80, 64), :]], axis=0)
    back_imag = jnp.concatenate([place_ref[pl.ds(160, 64), :], place_ref[pl.ds(240, 64), :]], axis=0)
    cosine, sine = turn_ref[0], turn_ref[1]
    return cosine * back_real + sine * back_imag, cosine * back_imag - sine * back_real


def columns(field_ref, out_ref):
    for y in range(2):
        for part in range(2):
            for plane in range(2):
                row = y * 4 + part * 2 + plane
                start = part * 128 + plane * 64 + y
                out_ref[:, row, :] = field_ref[pl.ds(start, SLABS, stride=2), :]


def unpack(got_ref, first_row, field_ref):
    for y in range(2):
        for part in range(2):
            for plane in range(2):
                row = y * 4 + part * 2 + plane
                start = part * 128 + plane * 64 + y
                field_ref[pl.ds(start, SLABS, stride=2), :] = got_ref[:, first_row + row, :]


def fetch(source_ref, boxes_ref, done):
    copy = pltpu.make_async_copy(source_ref, boxes_ref, done.at[0])
    copy.start()
    return copy


def coef_body(
    corner_ref, proj_ref, both_ref, next_ref, turn_ref, out_ref, field_ref, sums_ref, boxes_ref, done
):
    copy = fetch(corner_ref, boxes_ref, done)
    columns(both_ref, out_ref)
    for ahead, ref in enumerate((both_ref, next_ref)):
        turned_rows(
            ref[0:128, :], ref[128:256, :], turn_ref[2 * ahead], turn_ref[2 * ahead + 1], field_ref, 320 * ahead
        )
    copy.wait()
    coef = project(boxes_ref, proj_ref, 72, True, 32, field_ref, sums_ref)
    out_ref[:, 8:16, :] = jnp.broadcast_to(coef[None], (SLABS, 8, LANES))


def rest_body(
    corner_ref, shift_ref, proj_ref, table_ref, got_ref, turn_ref, local_ref, high_ref, low_ref,
    rest_ref, moved_ref, out_ref, place_ref, dual_ref, boxes_ref, done,
):
    copy = fetch(corner_ref, boxes_ref, done)
    field = got_ref[:, 0:8, :].reshape(256, LANES)
    moved = kinetic_x(field, high_ref, low_ref, shift_ref)
    moved_ref[...] = moved
    out_ref[:, 8:16, :] = moved.reshape(SLABS, 8, LANES)
    coef = first_coefs(lax.axis_index("fft"), got_ref)
    copy.wait()
    far_real, far_imag = spread(coef, boxes_ref, proj_ref, table_ref, turn_ref, place_ref, dual_ref)
    rest_ref[0:128, :] = local_ref[0:128, :] + far_real
    rest_ref[128:256, :] = local_ref[128:256, :] + far_imag
    columns(rest_ref, out_ref)


def first_body(
    corner_ref, shift_ref, proj_ref, got_ref, turn_ref, rest_ref, moved_ref, high_ref, low_ref,
    first_ref, out_ref, field_ref, sums_ref, boxes_ref, done,
):
    copy = fetch(corner_ref, boxes_ref, done)
    field = got_ref[:, 0:8, :].reshape(256, LANES) + moved_ref[...]
    out_ref[:, 0:8, :] = kinetic_x(field, high_ref, low_ref, shift_ref).reshape(SLABS, 8, LANES)
    unpack(got_ref, 8, first_ref)
    real = first_ref[0:128, :] + rest_ref[0:128, :]
    imag = first_ref[128:256, :] + rest_ref[128:256, :]
    first_ref[0:128, :] = real
    first_ref[128:256, :] = imag
    turned_rows(real, imag, turn_ref[0], turn_ref[1], field_ref, 0)
    copy.wait()
    coef = project(boxes_ref, proj_ref, 64, False, 4 * REACH, field_ref, sums_ref)
    out_ref[:, 8:16, :] = jnp.broadcast_to(coef[None], (SLABS, 8, LANES))


def final_body(
    corner_ref, shift_ref, proj_ref, table_ref, got_ref, turn_ref, both_ref, first_ref, pot_ref,
    y_high_ref, y_low_ref, z_high_ref, z_low_ref,
    new_ref, out_ref, field_ref, place_ref, dual_ref, boxes_ref, done,
):
    copy = fetch(corner_ref, boxes_ref, done)
    unpack(got_ref, 0, field_ref)
    coef = second_coefs(lax.axis_index("fft"), got_ref)
    copy.wait()
    far_real, far_imag = spread(coef, boxes_ref, proj_ref, table_ref, turn_ref, place_ref, dual_ref)
    half = 0.5 * time_step * time_step
    first = first_ref[...]
    near = kinetic_yz(first, (y_high_ref, y_low_ref), (z_high_ref, z_low_ref), shift_ref[2:3, :])
    pot = pot_ref[...]
    second_real = near[:128] + pot * first[:128] + field_ref[0:128, :] + far_real
    second_imag = near[128:] + pot * first[128:] + field_ref[128:256, :] + far_imag
    new_real = both_ref[0:128, :] + time_step * first_ref[128:256, :] - half * second_real
    new_imag = both_ref[128:256, :] - time_step * first_ref[0:128, :] - half * second_imag
    new_ref[0:128, :] = new_real
    new_ref[128:256, :] = new_imag
    weighted = shift_ref[1:2, :] * (new_real * new_real + new_imag * new_imag)
    weighted = weighted.reshape(2, BANDS, 4, LANES)
    for plane in range(2):
        out_ref[:, pl.ds(plane * 4, 4), :] = weighted[plane]


def tail_body(got_ref, new_ref, density_ref, real_hbm, imag_hbm, done):
    copies = [
        pltpu.make_async_copy(new_ref.at[pl.ds(0, 128)], real_hbm, done.at[0]),
        pltpu.make_async_copy(new_ref.at[pl.ds(128, 128)], imag_hbm, done.at[1]),
    ]
    for copy in copies:
        copy.start()
    density_ref[...] = jnp.sum(got_ref[...], axis=0)
    for copy in copies:
        copy.wait()


def smem():
    return pl.BlockSpec(memory_space=pltpu.SMEM)


def vmem():
    return pl.BlockSpec(memory_space=pltpu.VMEM)


def call(body, scalars, arrays, outs, scratch=(), cost=None):
    several = isinstance(outs, tuple)
    return pl.pallas_call(
        body,
        out_shape=outs,
        in_specs=[smem()] * len(scalars) + [vmem()] * len(arrays),
        out_specs=tuple(vmem() for _ in outs) if several else vmem(),
        scratch_shapes=list(scratch),
        compiler_params=pltpu.CompilerParams(vmem_limit_bytes=24 * 1024 * 1024),
        cost_estimate=cost,
    )(*scalars, *arrays)


def shape(*dims, dtype=f32):
    return jax.ShapeDtypeStruct(dims, dtype)


def exchange(value, axis):
    return lax.all_to_all(value, axis, split_axis=0, concat_axis=0, tiled=True)


def per_device(
    psi_real, psi_imag, potential, vector_potential, occupation, projectors, box_offsets, species, channels, coupling
):
    x_table, y_table, z_table = (jnp.asarray(table) for table in tables())
    real = psi_real.reshape(128, LANES)
    imag = psi_imag.reshape(128, LANES)
    pot = potential.reshape(128, LANES)
    matrix = jax.ShapeDtypeStruct((256, 256), jnp.bfloat16)
    corner = pltpu.SMEM((8, LANES), i32)
    signal = pltpu.SemaphoreType.DMA((1,))
    window = pltpu.VMEM((320, LANES), f32)
    square = pltpu.VMEM((128, LANES), f32)
    whole = pltpu.VMEM((256, LANES), f32)

    anywhere = pl.BlockSpec(memory_space=pltpu.HBM)
    slices, both = pl.pallas_call(
        pack_body,
        out_shape=(shape(8, 72, LANES), shape(256, LANES)),
        in_specs=[anywhere] * 6,
        out_specs=(vmem(), vmem()),
        scratch_shapes=[
            pltpu.SMEM((3, 4), i32), pltpu.SMEM((4,), i32), pltpu.SMEM((4, 8), i32),
            pltpu.VMEM((4, 8, 4096), f32), pltpu.VMEM((136, LANES), f32), pltpu.SemaphoreType.DMA((9,)),
        ],
        compiler_params=pltpu.CompilerParams(vmem_limit_bytes=60 * 1024 * 1024),
    )(box_offsets, species, channels, projectors, real, imag)
    ahead = lax.ppermute(both, "fft", [(i, (i + 24) % SLABS) for i in range(SLABS)])
    rows = [list(range(8 * x, 8 * x + 8)) for x in range(4)]
    got = lax.all_to_all(slices, "fft", split_axis=0, concat_axis=0, tiled=True, axis_index_groups=rows)
    turn, shift = call(phase_body, (vector_potential, occupation), (), (shape(4, 128, LANES), shape(8, LANES)))
    got, ahead, turn, shift = lax.optimization_barrier((got, ahead, turn, shift))
    chips = [[2 * y, 2 * y + 1] for y in range(8)]
    gathered = lax.all_gather(got, "band", axis_index_groups=chips)
    corners = call(pick_body, (), (got,), shape(8, LANES, dtype=i32))
    passed = lax.ppermute(got, "fft", [(i, (i + 8) % SLABS) for i in range(SLABS)])
    shares = call(
        coef_body, (), (corners, gathered.reshape(2, 576, LANES), both, ahead, turn), shape(SLABS, 16, LANES),
        (pltpu.VMEM((640, LANES), f32), square, corner, signal),
    )
    shares, passed, both = lax.optimization_barrier((shares, passed, both))
    local, high, low, *yz_split = call(
        local_body, (vector_potential,), (both, pot, x_table, y_table, z_table),
        (shape(256, LANES),) + (matrix,) * 6,
    )
    passed = lax.all_gather(passed, "band", axis_index_groups=chips)
    got = exchange(shares, "fft")
    beta, table, boxes = call(
        merge_body, (), (gathered, passed, coupling),
        (shape(2, 576, LANES), shape(64, LANES), shape(8, LANES, dtype=i32)),
    )
    rest, moved, shares = call(
        rest_body, (), (boxes, shift, beta, table, got, turn, local, high, low),
        (shape(256, LANES), shape(256, LANES), shape(SLABS, 16, LANES)), (window, square, corner, signal),
    )
    got = exchange(shares, "fft")
    first, shares = call(
        first_body, (), (boxes, shift, beta, got, turn, rest, moved, high, low),
        (shape(256, LANES), shape(SLABS, 16, LANES)), (window, square, corner, signal),
    )
    got = exchange(shares, "fft")
    new, weighted = call(
        final_body, (), (boxes, shift, beta, table, got, turn, both, first, pot, *yz_split),
        (shape(256, LANES), shape(BANDS, 8, LANES)), (whole, window, square, corner, signal),
    )
    density, new_real, new_imag = pl.pallas_call(
        tail_body,
        out_shape=(shape(8, LANES), shape(128, LANES), shape(128, LANES)),
        in_specs=[vmem()] * 2,
        out_specs=(vmem(), anywhere, anywhere),
        scratch_shapes=[pltpu.SemaphoreType.DMA((2,))],
        compiler_params=pltpu.CompilerParams(vmem_limit_bytes=24 * 1024 * 1024),
    )(exchange(weighted, "band"), new)
    density = density.reshape(2, 4, LANES)
    grid = (1, 2, NY, NZ)
    return new_real.reshape(grid), new_imag.reshape(grid), density


def solution(mesh):
    placed = (
        P("band", "fft", None, None),
        P("band", "fft", None, None),
        P("fft", None, None),
        P(),
        P("band"),
        P("fft", None, None),
        P(None, "fft"),
        P("fft"),
        P("fft", None),
        P(),
    )
    return jax.shard_map(
        per_device,
        mesh=mesh,
        in_specs=placed,
        out_specs=(
            P("band", "fft", None, None),
            P("band", "fft", None, None),
            P("fft", "band", None),
        ),
        check_vma=False,
    )
```
